32 devices in a mesh: group: 2 (over y), dm: 4 (over z), tm: 2 (over x), beam: 2 (over core).
Axes of the slice: x: 2, y: 2, z: 4, core: 2. Of those that a mesh axis runs over, the one named last changes fastest.
Arguments:
- raw: bfloat16 [16, 4194304], P(('group', 'dm', 'beam'), 'tm'), parts along dimension 0
- proto: float32 [4, 16384], replicated, may hold values from -4 to 4
- delays: int32 [8, 4, 64], replicated, may hold values from 0 to 3, as said below
- widths: int32 [8], replicated, may hold values from 1 to 8, as said below
- owners: int32 [8, 1], replicated, may hold values from 0 to 3; in each aligned block of 8 rows (0 to 7, 8 to 15, ...) at most 4 rows name the same one
Outputs:
- detect: bfloat16 [16, 8, 2, 4, 8, 256], P('dm', 'group', 'beam', None, None, 'tm'), parts along dimension 1
The draws below stay inside these ranges and needn't reach their ends.
There are 2 independent parts, one for each index of `group`. The reference program is written for one: setup_inputs(seed, part) draws one part's arguments, and reference() takes and returns one part's arrays. A program takes and returns all parts, laid end to end along the dimension named above; an argument that names none is the same for every part. Nothing has to cross between parts.
Inputs may be any that keep to these rules, and one draw needn't show every extreme that they name: `delays`: 3 occurs in every draw. `widths`: 8 occurs in every draw. `owners`: each owner holds at most 4 DM blocks, and some owner holds exactly 4.
All inputs are finite; a program needn't handle non-finite values.
Results may differ from the reference program's by a relative error of at most 0.014.
Values may be sent and summed in bfloat16 or wider, within the bound.
A program may use at most 128 MiB of HBM per device.

```python
import math
import jax
import jax.numpy as jnp
import numpy as np
from jax import lax

NCH = 16384
DFT_A = 128
DFT_B = 128
TAPS = 4
NBLK = 64
CBW = 256
SPECTRA = 256
SAMPLES = 4194304
BEAM_SUB = 2
BEAMS = 8
PFB_BLK = 16
FD = 4
TT = 8
MAXT = 3
WMAX = 8
NBOX = 8
TRIALS = 4
NDMB = 8
CAP = 4
SLOTS = 16
HALO = 31
N_DM = 4


def draw_raw(key, part):
    key_noise = jax.random.fold_in(key, 11)
    key_level = jax.random.fold_in(key, 12)
    steps = jnp.arange(SPECTRA, dtype=jnp.float32) / max(SPECTRA - 1, 1)
    jitter = jax.random.uniform(key_level, (BEAMS, SPECTRA, 1), jnp.float32)
    values = jax.random.normal(key_noise, (BEAMS, SPECTRA, NCH), jnp.float32)
    level = jnp.power(10.0, 0.5 * steps[None, :, None] + 0.5 * jitter)
    return (values * jnp.sqrt(level)).reshape(BEAMS, SAMPLES).astype(jnp.bfloat16)


def draw_delays(key, part):
    block = jnp.arange(NDMB, dtype=jnp.int32)[:, None, None]
    trial = jnp.arange(TRIALS, dtype=jnp.int32)[None, :, None]
    channel = jnp.arange(NBLK, dtype=jnp.int32)[None, None, :]
    level = block * TRIALS + trial
    base = level * (NBLK - 1 - channel) * MAXT // max((NDMB * TRIALS - 1) * (NBLK - 1), 1)
    jitter = jax.random.randint(jax.random.fold_in(key, 21), (NDMB, TRIALS, NBLK), 0, 2)
    return jnp.minimum(base + jitter, MAXT).astype(jnp.int32)


def draw_widths(key, part):
    values = jax.random.randint(jax.random.fold_in(key, 31), (NBOX,), 1, WMAX + 1)
    where_top = jax.random.randint(jax.random.fold_in(key, 32), (), 0, NBOX)
    index = jnp.arange(NBOX, dtype=jnp.int32)
    return jnp.where(index == where_top, WMAX, values).astype(jnp.int32)


def shared_out(own_key, own, number, rows, amount, top, reach, skew):
    sequence = jax.random.permutation(own_key, amount)
    packed, usual = portions_of(amount, rows * top, reach, skew, True), portions_of(amount, rows * top, reach, skew, False)
    places = jnp.arange(amount)

    def named(tallies, rotation):
        used = int((tallies > 0).sum())
        fixed = max(1, used // 4)
        moved = fixed + (places - fixed + rotation * (used - fixed)) % max(1, amount - fixed)
        return jnp.zeros((amount,), jnp.int32).at[sequence[jnp.where(places < fixed, places, moved)]].set(jnp.asarray(tallies, jnp.int32))

    tallies = jnp.where(number % 4 == 0, named(packed, number // 4), named(usual, number - number // 4 - 1))
    mixed = jax.random.permutation(jax.random.fold_in(own, 3), amount)
    donor, taker = mixed[0:amount // 2 * 2:2], mixed[1:amount // 2 * 2:2]
    room = jnp.minimum(tallies[donor] - 1, reach - tallies[taker]) // 2
    room = jnp.where((donor == sequence[0]) | (taker == sequence[0]) | (tallies[taker] == 0), 0, jnp.maximum(room, 0))
    moved = jax.random.randint(jax.random.fold_in(own, 4), (amount // 2,), 0, 1 << 20) % (room + 1)
    tallies = tallies.at[donor].add(-moved).at[taker].add(moved)
    members = jnp.searchsorted(jnp.cumsum(tallies), jnp.arange(rows * top), side="right").astype(jnp.int32)
    table = members.reshape(top, rows).T
    table = table[jax.random.permutation(jax.random.fold_in(own, 1), rows)]
    rotation = jax.random.randint(jax.random.fold_in(own, 2), (rows, 1), 0, top)
    return jnp.take_along_axis(table, (jnp.arange(top)[None, :] + rotation) % top, axis=1)


def portions_of(number_of, total, bound, skew, full):
    weights = [(1 << 20) // math.isqrt(rank ** skew) + 1 for rank in range(1, number_of + 1)]
    largest = bound if full else min(bound, max(-(-total // number_of), total * weights[0] // sum(weights)))
    least = 1 if total - largest >= number_of - 1 else 0
    counts, rest = [largest] + [least] * (number_of - 1), total - largest - least * (number_of - 1)
    while rest > 0:
        candidates = [i for i in range(1, number_of) if counts[i] < largest] or [i for i in range(1, number_of) if counts[i] < bound]
        pool, budget = sum([weights[i] for i in candidates]), rest
        for i in candidates:
            more = min(bound - counts[i], max(1, budget * weights[i] // pool), rest)
            counts[i] = counts[i] + more
            rest = rest - more
    return np.array(counts)


def centred(rng, shape, scale, bound, held_as=jnp.bfloat16):
    values = jax.random.normal(rng, shape, jnp.float32) * scale
    return jnp.minimum(jnp.maximum(values, -bound), bound).astype(held_as)


def setup_inputs(seed: int = 0, part: int = 0) -> dict:
    seeds = jax.random.split(jax.random.key(seed), 6)
    part_keys = jax.random.split(jax.random.fold_in(seeds[5], part), 6)
    raw = draw_raw(jax.random.fold_in(jax.random.fold_in(seeds[5], part), 71), part)
    proto = centred(seeds[1], (TAPS, NCH), 1.0, 4.0, jnp.float32)
    delays = draw_delays(jax.random.fold_in(seeds[5], 71), part)
    widths = draw_widths(jax.random.fold_in(seeds[5], 71), part)
    owners_keys = jax.random.split(jax.random.fold_in(seeds[4], 1), NDMB // NDMB)
    owners_turns = jax.random.permutation(jax.random.fold_in(seeds[4], 3), NDMB // NDMB)
    owners = jax.vmap(lambda own, number: shared_out(jax.random.fold_in(seeds[4], 2), own, number, NDMB, N_DM, 1, CAP, 2))(owners_keys, owners_turns).reshape((NDMB, 1))
    return dict(raw=raw, proto=proto, delays=delays, widths=widths, owners=owners)


def dft_tables(size):
    index = jnp.arange(size, dtype=jnp.int32)
    product = index[:, None] * index[None, :] % size
    angle = product.astype(jnp.float32) * (2.0 * math.pi / size)
    return (jnp.cos(angle).astype(jnp.bfloat16), jnp.sin(angle).astype(jnp.bfloat16))

def twiddle_tables(rows, cols, total):
    first = jnp.arange(rows, dtype=jnp.int32)
    second = jnp.arange(cols, dtype=jnp.int32)
    product = first[:, None] * second[None, :] % total
    angle = product.astype(jnp.float32) * (2.0 * math.pi / total)
    return (jnp.cos(angle), jnp.sin(angle))

def spectra_power(window_frames, proto):
    count = window_frames.shape[0] - TAPS + 1
    hp = lax.Precision.HIGHEST
    acc = window_frames[0:count].astype(jnp.float32) * proto[0]
    for tap in range(1, TAPS):
        acc = acc + window_frames[tap:tap + count].astype(jnp.float32) * proto[tap]
    frames_bf = acc.astype(jnp.bfloat16).astype(jnp.float32).reshape(count, DFT_A, DFT_B)
    cos_a, sin_a = dft_tables(DFT_A)
    cos_b, sin_b = dft_tables(DFT_B)
    tw_cos, tw_sin = twiddle_tables(DFT_B, DFT_A, NCH)
    a_re = jnp.einsum('kab,fa->kbf', frames_bf, cos_a.astype(jnp.float32), precision=hp)
    a_im = -jnp.einsum('kab,fa->kbf', frames_bf, sin_a.astype(jnp.float32), precision=hp)
    t_re = (a_re * tw_cos + a_im * tw_sin).astype(jnp.bfloat16).astype(jnp.float32)
    t_im = (a_im * tw_cos - a_re * tw_sin).astype(jnp.bfloat16).astype(jnp.float32)
    cb = cos_b.astype(jnp.float32)
    sb = sin_b.astype(jnp.float32)
    c_re = jnp.einsum('kbf,gb->kgf', t_re, cb, precision=hp) + jnp.einsum('kbf,gb->kgf', t_im, sb, precision=hp)
    c_im = jnp.einsum('kbf,gb->kgf', t_im, cb, precision=hp) - jnp.einsum('kbf,gb->kgf', t_re, sb, precision=hp)
    power = (c_re * c_re + c_im * c_im) * (1.0 / (TAPS * NCH))
    return power.reshape(count, NCH)

def fine_masks(groups, width):
    block = jnp.arange(groups, dtype=jnp.int32)[:, None]
    inner = jnp.arange(width, dtype=jnp.int32)[None, :]
    fine = block * FD * (width - 1 - inner) // (groups * (width - 1))
    return jnp.stack([(fine == step).astype(jnp.float32) for step in range(FD)])

def beam_subbands(samples, proto, masks):
    frames = samples.reshape(SPECTRA, NCH)
    padded = jnp.concatenate([jnp.zeros((TAPS - 1, NCH), jnp.bfloat16), frames], 0)

    def block_power(index):
        start = (index * PFB_BLK).astype(jnp.int32)
        window = lax.dynamic_slice_in_dim(padded, start, PFB_BLK + TAPS - 1, 0)
        return spectra_power(window, proto)
    power = lax.map(block_power, jnp.arange(SPECTRA // PFB_BLK, dtype=jnp.int32)).reshape(SPECTRA, NCH)
    band = lax.optimization_barrier(jnp.sum(power, 0)) / SPECTRA
    ratio = power / (band + 1e-06)
    flat = (ratio - lax.optimization_barrier(jnp.mean(ratio, 1, keepdims=True))).astype(jnp.bfloat16)
    flat = jnp.concatenate([jnp.zeros((FD - 1, NCH), jnp.bfloat16), flat], 0)
    view = flat.reshape(SPECTRA + FD - 1, NBLK, CBW).astype(jnp.float32)
    total = jnp.zeros((NDMB, NBLK, SPECTRA), jnp.float32)
    for step in range(FD):
        part = view[FD - 1 - step:FD - 1 - step + SPECTRA]
        total = total + jnp.einsum('kci,gi->gck', part, masks[step], precision=lax.Precision.HIGHEST)
    return (total * (1.0 / math.sqrt(CBW))).astype(jnp.bfloat16)

def dedisperse(extended, delays, count):
    length = count + WMAX - 1
    total = 0.0
    for value in range(MAXT + 1):
        start = (MAXT - value) * TT
        window = extended[..., start:start + length].astype(jnp.float32)
        mask = (delays == value).astype(jnp.float32)
        total = total + jnp.einsum('rgck,gjc->rgjk', window, mask, precision=lax.Precision.HIGHEST)
    return total * (1.0 / math.sqrt(NBLK))

def boxcar(series, widths, count):
    lags = jnp.arange(WMAX, dtype=jnp.int32)
    weights = (lags[None, :] < widths[:, None]).astype(jnp.float32) / jnp.sqrt(widths.astype(jnp.float32))[:, None]
    stacked = jnp.stack([series[..., WMAX - 1 - lag:WMAX - 1 - lag + count] for lag in range(WMAX)], -2)
    return jnp.einsum('rgjik,wi->rgjwk', stacked, weights, precision=lax.Precision.HIGHEST)

def slot_table(owners, owner_count, capacity):
    owner = owners[:, 0]
    groups = owner.shape[0]
    index = jnp.arange(groups, dtype=jnp.int32)
    same = owner[:, None] == owner[None, :]
    earlier = index[None, :] < index[:, None]
    rank = lax.optimization_barrier(jnp.sum((same & earlier).astype(jnp.int32), 1))
    hit_owner = owner[None, None, :] == jnp.arange(owner_count, dtype=jnp.int32)[:, None, None]
    hit_slot = rank[None, None, :] == jnp.arange(capacity, dtype=jnp.int32)[None, :, None]
    return (hit_owner & hit_slot).astype(jnp.int32)

def reference(raw, proto, delays, widths, owners):
    masks = fine_masks(NDMB, CBW)

    def one_beam(samples):
        return beam_subbands(samples, proto, masks)
    subs = lax.map(one_beam, raw)
    extended = jnp.concatenate([jnp.zeros((BEAMS, NDMB, NBLK, HALO), jnp.bfloat16), subs], -1)
    series = dedisperse(extended, delays, SPECTRA)
    box = boxcar(series, widths, SPECTRA).astype(jnp.bfloat16)
    table = slot_table(owners, N_DM, CAP).astype(jnp.float32)
    placed = jnp.einsum('osg,rgjwk->osrjwk', table, box.astype(jnp.float32), precision=lax.Precision.HIGHEST)
    return placed.reshape(SLOTS, N_DM, BEAM_SUB, TRIALS, NBOX, SPECTRA).astype(jnp.bfloat16)
```

```python
import functools
import math

import jax
import jax.numpy as jnp
import numpy as np
from jax import lax
from jax.experimental import pallas as pl
from jax.experimental.pallas import tpu as pltpu
from jax.sharding import PartitionSpec as P

SIDE = 128
NBLK = 64
FD = 4
TT = 8
MAXT = 3
WMAX = 8
SPB = 32
FIRST = 4
PIECE = 16
HALF = SIDE // 2
FR = 72
BACK = 128 - TT
MESH = pl.DeviceIdType.MESH
F32 = jnp.float32
BF16 = jnp.bfloat16


def tables(channels):
    i = np.arange(SIDE)
    ang = (i[:, None] * i[None, :] % SIDE) * (2.0 * math.pi / SIDE)
    c, s = np.cos(ang), np.sin(ang)
    w1 = np.concatenate([c[:FR], s[:FR]], 0)
    w2 = np.block([[c, -s], [-s, -c]])
    tw = (i[:, None] * i[None, :] % channels) * (2.0 * math.pi / channels)
    twiddle = np.stack([np.cos(tw[:FR]), np.sin(tw[:FR])]).astype(np.float32)
    return jnp.asarray(w1, BF16), jnp.asarray(w2, BF16), jnp.asarray(twiddle)


def fine_rows(groups, width):
    g = np.arange(groups)[:, None]
    i = np.arange(width)[None, :]
    fine = g * FD * (width - 1 - i) // (groups * (width - 1))
    hot = np.stack([fine == step for step in range(FD)])
    hot = hot.reshape(FD, groups, width // SIDE, SIDE).transpose(2, 0, 1, 3)
    out = np.zeros((2, 2, FD, groups, FR))
    out[0, ..., : HALF + 1] = hot[..., : HALF + 1]
    out[1, ..., 1:HALF] = hot[..., : HALF : -1]
    return jnp.asarray(out.reshape(-1, FR), BF16)


def iota(shape, dim):
    return lax.broadcasted_iota(jnp.int32, shape, dim)


def search_kernel(
    sizes, raw_ref, proto_ref, w1_any, w2_any, tw_any, m_any, delays_any, widths_any, owners_any, out_ref,
    xbuf, proto, w1_ref, w2_ref, tw_ref, m_ref, delays_ref, widths_ref, owners_ref,
    win, history, p_ref, band_ref, bands, inv, direct, mirror, send, sendb, got, gotb,
    raw_sem, proto_sem, const_sem,
    hist_send, hist_recv, band_send, band_recv, own_send, own_recv, next_send, next_recv,
):
    spectra, spec, groups, slabs, owner_count, axes = sizes
    frame = SIDE * SIDE
    slots = out_ref.shape[0]
    boxes = widths_ref.shape[1]
    trials = out_ref.shape[2] // boxes
    quad = trials * groups
    rows = slots * trials
    tm, dm = lax.axis_index("tm"), lax.axis_index("dm")

    def peer(slab, owner):
        place = {name: lax.axis_index(name) for name in axes}
        place["tm"] = lax.rem(tm + slab, slabs)
        place["dm"] = lax.rem(dm + owner, owner_count)
        return tuple(place[name] for name in axes)

    def remote(src, dst, send_sem, recv_sem, target):
        return pltpu.make_async_remote_copy(
            src_ref=src, dst_ref=dst, send_sem=send_sem, recv_sem=recv_sem,
            device_id=target, device_id_type=MESH,
        )

    def raw_copy(piece):
        part = pl.ds(pl.multiple_of(piece * PIECE * frame, PIECE * frame), PIECE * frame)
        return pltpu.make_async_copy(raw_ref.at[:, part], xbuf.at[:, part], raw_sem.at[piece])

    def history_copy():
        size = history.shape[1]
        last = raw_ref.at[:, pl.ds(spec * frame - size, size)]
        return remote(last, history, hist_send, hist_recv, peer(1, 0))

    barrier = pltpu.get_barrier_semaphore()
    senders = [(off, 0) for off in range(1, slabs)] + [(0, off) for off in range(1, owner_count)]
    if slabs > 1:
        senders += [(slabs - 1, off) for off in range(1, owner_count)]
    for slab, owner in senders:
        pl.semaphore_signal(barrier, inc=1, device_id=peer(slab, owner), device_id_type=MESH)

    constants = [
        pltpu.make_async_copy(src, dst, const_sem.at[n])
        for n, (src, dst) in enumerate(
            [
                (w1_any, w1_ref), (tw_any, tw_ref), (w2_any, w2_ref), (m_any, m_ref),
                (delays_any, delays_ref), (widths_any, widths_ref), (owners_any, owners_ref),
            ]
        )
    ]
    taps = [
        pltpu.make_async_copy(proto_ref.at[tap : tap + 1], proto.at[tap], proto_sem.at[tap])
        for tap in range(4)
    ]
    raw_copy(0).start()
    for copy in taps:
        copy.start()
    constants[0].start()
    constants[1].start()
    constants[2].start()
    raw_copy(1).start()
    for copy in constants[3:]:
        copy.start()
    for piece in range(2, spec // PIECE):
        raw_copy(piece).start()
    band_ref[...] = jnp.zeros_like(band_ref)

    def unfold(ref, start):
        return ref[:, pl.ds(start, frame)].reshape(SIDE, SIDE).astype(F32)

    def fill(base, k):
        start = pl.multiple_of((base + k) * frame, frame)
        row = pl.multiple_of((base + k + 3) * SIDE, SIDE)
        win[pl.ds(row, SIDE)] = unfold(xbuf, start)

    def pair(base, s):
        ys = []
        for k in (s, s + 1):
            acc = 0.0
            for tap in range(4):
                row = pl.multiple_of((base + k + tap) * SIDE, SIDE)
                acc = acc + win[pl.ds(row, SIDE)] * proto[tap].reshape(SIDE, SIDE)
            ys.append(acc.astype(BF16))
        a = jnp.dot(w1_ref[...], jnp.concatenate(ys, 1), preferred_element_type=F32)
        res, ims = [], []
        for m in range(2):
            re = a[:FR, m * SIDE : (m + 1) * SIDE]
            im = a[FR:, m * SIDE : (m + 1) * SIDE]
            res.append(re * tw_ref[0] - im * tw_ref[1])
            ims.append(im * tw_ref[0] + re * tw_ref[1])
        t = jnp.concatenate(
            [jnp.concatenate(res, 0).astype(BF16), jnp.concatenate(ims, 0).astype(BF16)], 1
        )
        c = jnp.dot(t, w2_ref[...], preferred_element_type=F32)
        re, im = c[:, :SIDE], c[:, SIDE:]
        power = re * re + im * im
        p_ref[pl.ds(pl.multiple_of((base + s) * FR, FR), 2 * FR)] = power
        band_ref[...] += power[:FR] + power[FR:]

    raw_copy(0).wait()
    for copy in taps:
        copy.wait()
    for copy in constants[:3]:
        copy.wait()
    for k in range(PIECE):
        fill(0, k)
    for s in range(FIRST, PIECE, 2):
        pair(0, s)
    raw_copy(1).wait()
    for k in range(PIECE, SPB):
        fill(0, k)
    for s in range(PIECE, SPB, 2):
        pair(0, s)

    pl.semaphore_wait(barrier, len(senders))
    if slabs > 1:
        history_copy().start()

    def chunk(step, carry):
        base = step * SPB
        for piece in range(SPB // PIECE):
            raw_copy(step * (SPB // PIECE) + piece).wait()
        for k in range(SPB):
            fill(base, k)
        for s in range(0, SPB, 2):
            pair(base, s)
        return carry

    lax.fori_loop(1, spec // SPB, chunk, 0)

    if slabs > 1:
        history_copy().wait()
        for k in range(3):
            win[k * SIDE : (k + 1) * SIDE] = jnp.where(tm > 0, unfold(history, k * frame), 0.0)
    else:
        win[: 3 * SIDE] = jnp.zeros((3 * SIDE, SIDE), F32)
    for s in range(0, FIRST, 2):
        pair(0, s)

    copies = []
    for off in range(1, slabs):
        copy = remote(band_ref, bands.at[off - 1], band_send.at[off - 1], band_recv.at[off - 1], peer(off, 0))
        copy.start()
        copies.append(copy)

    for copy in constants[3:]:
        copy.wait()
    lanes = (MAXT + 1) * quad
    spot = iota((NBLK, SIDE), 0)
    lane = iota((NBLK, SIDE), 1) // 2
    spread = jnp.concatenate([lane == spot, lane == NBLK - 1 - spot], 1).astype(F32).astype(BF16)
    late = jnp.dot(delays_ref[...].astype(F32).astype(BF16), spread, preferred_element_type=F32)
    line = iota((quad, 2 * SIDE), 0) // trials
    masks = [
        jnp.concatenate(
            [
                jnp.where((late == float(v)) & (line == g), 1.0, 0.0)
                for v in range(MAXT + 1)
            ],
            0,
        ).astype(BF16)
        for g in range(groups)
    ]

    def column(ref):
        n = ref.shape[1]
        same = iota((n, n), 0) == iota((n, n), 1)
        return jnp.sum(jnp.where(same, jnp.broadcast_to(ref[...], (n, n)), 0), 1, keepdims=True)

    lane = iota((groups, lanes), 1) % quad
    row = iota((groups, lanes), 0)
    owner = jnp.broadcast_to(column(owners_ref), (groups, lanes))
    mine = jnp.sum(jnp.where(lane // trials == row, owner, 0), 0, keepdims=True)
    rank = jnp.sum(jnp.where((owner == mine) & (row < lane // trials), 1, 0), 0, keepdims=True)
    place = (mine * slots + rank) * trials + lane[:1] % trials
    pack = jnp.where(iota((owner_count * rows, lanes), 0) == place, 1.0, 0.0)
    pack = jnp.concatenate([pack, pack], 1).astype(BF16)

    reach = jnp.broadcast_to(column(widths_ref), (boxes, SIDE))
    root = 1.0 / jnp.sqrt(reach.astype(F32))
    root = jnp.concatenate([root] * rows, 0)
    reach = jnp.concatenate([reach] * rows, 0)
    if WMAX * rows > SIDE:
        reach = jnp.broadcast_to(reach[:, :1], (boxes * rows, WMAX * rows))
    lag = iota((boxes * rows, WMAX * rows), 1)
    series = iota((boxes * rows, WMAX * rows), 0) // boxes
    kernel = jnp.where((lag % rows == series) & (lag // rows < reach), 1.0, 0.0)
    kernel = jnp.concatenate([kernel, kernel], 1).astype(BF16)
    direct[spec + FD - 1 :] = jnp.zeros((direct.shape[0] - spec - FD + 1, groups, SIDE), F32)
    mirror[spec + FD - 1 :] = jnp.zeros((direct.shape[0] - spec - FD + 1, groups, SIDE), F32)

    band = band_ref[...]
    for off in range(1, slabs):
        copies[off - 1].wait()
        band = band + bands[off - 1]
    scale = 1.0 / (4 * frame)
    held = iota((FR, SIDE), 0) <= HALF
    inv[...] = jnp.where(held, scale / (band * (scale / spectra) + 1e-06), 0.0)

    even = iota((FD * groups, SIDE), 1) % 2 == 0
    size = FD * groups

    def block(step, carry):
        carry = list(carry)
        for s in range(0, SPB, 2):
            flats = []
            for k in (s, s + 1):
                start = pl.multiple_of((step * SPB + k) * FR, FR)
                ratio = p_ref[pl.ds(start, FR)] * inv[...]
                total = 2.0 * jnp.sum(ratio, 0, keepdims=True) - ratio[:1] - ratio[HALF : HALF + 1]
                mean = jnp.sum(total, 1, keepdims=True) * (1.0 / frame)
                flats.append((ratio - mean).astype(BF16))
            r = jnp.dot(m_ref[...], jnp.concatenate(flats, 1), preferred_element_type=F32)
            for m in range(2):
                part = r[:, m * SIDE : (m + 1) * SIDE]
                one = jnp.where(even, part[:size], part[size : 2 * size])
                two = jnp.where(even, part[3 * size :], part[2 * size : 3 * size])
                for n, (ref, new) in enumerate(((direct, one), (mirror, two))):
                    new = [new[d * groups : (d + 1) * groups] for d in range(FD)]
                    held = carry[n * (FD - 1) : (n + 1) * (FD - 1)] + [0.0]
                    ref[step * SPB + s + m] = held[0] + new[0]
                    for d in range(1, FD):
                        carry[n * (FD - 1) + d - 1] = held[d] + new[d]
        return tuple(carry)

    zero = jnp.zeros((groups, SIDE), F32)
    carry = lax.fori_loop(0, spec // SPB, block, (zero,) * (2 * (FD - 1)))
    for d in range(FD - 1):
        direct[spec + d] = carry[d]
        mirror[spec + d] = carry[FD - 1 + d]

    count = direct.shape[0]
    each = 0.0
    for g in range(groups):
        both = jnp.concatenate([direct[:, g, :], mirror[:, g, :]], 1).astype(BF16)
        each = each + lax.dot_general(
            both, masks[g], (((1,), (1,)), ((), ())), preferred_element_type=F32
        )
    length = count + MAXT * TT
    value = iota((length, lanes), 1) // quad
    dd = 0.0
    for v in range(MAXT + 1):
        pads = [jnp.zeros((v * TT, lanes), F32), each, jnp.zeros(((MAXT - v) * TT, lanes), F32)]
        moved = jnp.concatenate([part for part in pads if part.shape[0]], 0)
        dd = jnp.where(value == v, moved, dd)
    dd = dd * (1.0 / math.sqrt(SIDE * SIDE // NBLK) / math.sqrt(NBLK))
    back = spec - TT
    dd = jnp.concatenate([dd[:spec], dd[back:], jnp.zeros((SIDE - length + back, lanes), F32)], 0)
    high = dd.astype(BF16)
    low = (dd - high.astype(F32)).astype(BF16)
    packed = lax.dot_general(
        pack, jnp.concatenate([high, low], 1), (((1,), (1,)), ((), ())), preferred_element_type=F32
    )
    send[...] = packed[:, :spec].reshape(send.shape)
    sendb[...] = packed[:, spec:].reshape(sendb.shape)

    copies = []
    for off in range(1, owner_count):
        copy = remote(
            send.at[lax.rem(dm + off, owner_count)], got.at[dm],
            own_send.at[off - 1], own_recv.at[off - 1], peer(0, off),
        )
        copy.start()
        copies.append(copy)
    if slabs > 1:
        for off in range(owner_count):
            copy = remote(
                sendb.at[lax.rem(dm + off, owner_count)], gotb.at[dm],
                next_send.at[off], next_recv.at[off], peer(1, off),
            )
            copy.start()
            copies.append(copy)
    got[dm] = send[dm]
    for copy in copies:
        copy.wait()

    lane = iota((rows, SIDE), 1)
    stacks = []
    for d in range(owner_count):
        own = got[d]
        if slabs > 1:
            before = jnp.where(tm > 0, gotb[d], 0.0)
            own = own + jnp.where(lane < SIDE - TT, pltpu.roll(before, SIDE - TT, 1), 0.0)
            past = pltpu.roll(before, SIDE - TT, 1)
        else:
            past = jnp.zeros((rows, SIDE), F32)
        moved = [own]
        for lag in range(1, WMAX):
            moved.append(jnp.where(lane < lag, pltpu.roll(past, lag, 1), pltpu.roll(own, lag, 1)))
        stacks.append(jnp.concatenate(moved, 0))
    stack = jnp.concatenate(stacks, 1)
    high = stack.astype(BF16)
    low = (stack - high.astype(F32)).astype(BF16)
    box = jnp.dot(kernel, jnp.concatenate([high, low], 0), preferred_element_type=F32)
    for d in range(owner_count):
        done = (box[:, d * SIDE : (d + 1) * SIDE] * root).astype(BF16)
        for s in range(slots):
            out_ref[s, d] = done[s * trials * boxes : (s + 1) * trials * boxes]


def shards(axes, raw, proto, delays, widths, owners):
    taps, channels = proto.shape
    spec = raw.shape[1] // channels
    groups, trials, _ = delays.shape
    slabs, owner_count = lax.axis_size("tm"), lax.axis_size("dm")
    capacity = 2 * (groups // owner_count)
    w1, w2, tw = tables(channels)
    masks = fine_rows(groups, channels // NBLK)
    sizes = (spec * slabs, spec, groups, slabs, owner_count, axes)
    rows = -(-(spec + FD - 1) // 8) * 8
    block = pltpu.VMEM((owner_count, capacity * trials, SIDE), F32)
    sems = lambda n: pltpu.SemaphoreType.DMA((max(n, 1),))
    small = [w1, w2, tw, masks, delays.reshape(groups * trials, NBLK), widths[None], owners.T]
    out = (capacity, owner_count, trials * widths.shape[0], spec)
    box = pl.pallas_call(
        functools.partial(search_kernel, sizes),
        in_specs=[pl.BlockSpec(memory_space=pl.ANY)] * (2 + len(small)),
        out_specs=pl.BlockSpec(memory_space=pltpu.VMEM),
        out_shape=jax.ShapeDtypeStruct(out, BF16),
        scratch_shapes=[
            pltpu.VMEM((1, spec * channels), BF16),
            pltpu.VMEM((taps, 1, channels), F32),
            *[pltpu.VMEM(value.shape, value.dtype) for value in small],
            pltpu.VMEM(((spec + 3) * SIDE, SIDE), F32),
            pltpu.VMEM((1, 3 * channels), BF16),
            pltpu.VMEM((spec * FR, SIDE), F32),
            pltpu.VMEM((FR, SIDE), F32),
            pltpu.VMEM((max(slabs - 1, 1), FR, SIDE), F32),
            pltpu.VMEM((FR, SIDE), F32),
            pltpu.VMEM((rows, groups, SIDE), F32),
            pltpu.VMEM((rows, groups, SIDE), F32),
            block,
            block,
            block,
            block,
            sems(spec // PIECE),
            sems(taps),
            sems(len(small)),
            pltpu.SemaphoreType.DMA,
            pltpu.SemaphoreType.DMA,
            sems(slabs - 1),
            sems(slabs - 1),
            sems(owner_count - 1),
            sems(owner_count - 1),
            sems(owner_count),
            sems(owner_count),
        ],
        compiler_params=pltpu.CompilerParams(
            vmem_limit_bytes=56 << 20, collective_id=0, has_side_effects=True
        ),
        name="search",
    )(raw, proto, *small)
    return box.reshape(capacity, owner_count, 1, trials, widths.shape[0], spec)


def solution(mesh):
    return jax.shard_map(
        functools.partial(shards, mesh.axis_names),
        mesh=mesh,
        in_specs=(P(("group", "dm", "beam"), "tm"), P(), P(), P(), P()),
        out_specs=P("dm", "group", "beam", None, None, "tm"),
        check_vma=False,
    )
```

```python
import functools
import math

import jax
import jax.numpy as jnp
import numpy as np
from jax import lax
from jax.experimental import pallas as pl
from jax.experimental.pallas import tpu as pltpu
from jax.sharding import PartitionSpec as P

SIDE = 128
NBLK = 64
FD = 4
TT = 8
MAXT = 3
WMAX = 8
SPB = 32
FIRST = 4
CHUNK = 16
GROUP = 4
HALF = SIDE // 2
FR = 72
BACK = 128 - TT
MESH = pl.DeviceIdType.MESH
F32 = jnp.float32
BF16 = jnp.bfloat16
FT = BF16


def tables(channels):
    i = np.arange(SIDE)
    ang = (i[:, None] * i[None, :] % SIDE) * (2.0 * math.pi / SIDE)
    c, s = np.cos(ang), np.sin(ang)
    w1 = np.concatenate([c[:FR], s[:FR]], 0)
    w2 = np.block([[c, -s], [-s, -c]])
    tw = (i[:, None] * i[None, :] % channels) * (2.0 * math.pi / channels)
    twiddle = np.stack([np.cos(tw[:FR]), np.sin(tw[:FR])]).astype(np.float32)
    return jnp.asarray(w1, BF16), jnp.asarray(w2, BF16), jnp.asarray(twiddle)


def fine_rows(groups, width):
    g = np.arange(groups)[:, None]
    i = np.arange(width)[None, :]
    fine = g * FD * (width - 1 - i) // (groups * (width - 1))
    hot = np.stack([fine == step for step in range(FD)])
    hot = hot.reshape(FD, groups, width // SIDE, SIDE).transpose(2, 0, 1, 3)
    out = np.zeros((2, 2, FD, groups, FR))
    out[0, ..., : HALF + 1] = hot[..., : HALF + 1]
    out[1, ..., 1:HALF] = hot[..., : HALF : -1]
    return jnp.asarray(out.reshape(-1, FR), BF16)


def iota(shape, dim):
    return lax.broadcasted_iota(jnp.int32, shape, dim)


def search_kernel(
    sizes, raw_ref, proto_ref, w1_any, w2_any, tw_any, m_any, delays_any, widths_any, owners_any, out_ref,
    xbuf, proto, w1_ref, w2_ref, tw_ref, m_ref, delays_ref, widths_ref, owners_ref,
    yone, ytwo, history, p_ref, band_ref, bands, inv, direct, mirror, send, sendb, got, gotb,
    raw_sem, proto_sem, const_sem,
    hist_send, hist_recv, band_send, band_recv, own_send, own_recv, next_send, next_recv,
):
    spectra, spec, groups, slabs, owner_count, axes = sizes
    frame = SIDE * SIDE
    slots = out_ref.shape[0]
    boxes = widths_ref.shape[1]
    trials = out_ref.shape[2] // boxes
    quad = trials * groups
    rows = slots * trials
    tm, dm = lax.axis_index("tm"), lax.axis_index("dm")

    def peer(slab, owner):
        place = {name: lax.axis_index(name) for name in axes}
        place["tm"] = lax.rem(tm + slab, slabs)
        place["dm"] = lax.rem(dm + owner, owner_count)
        return tuple(place[name] for name in axes)

    def remote(src, dst, send_sem, recv_sem, target):
        return pltpu.make_async_remote_copy(
            src_ref=src, dst_ref=dst, send_sem=send_sem, recv_sem=recv_sem,
            device_id=target, device_id_type=MESH,
        )

    def raw_copy(piece):
        start = pl.multiple_of(piece * CHUNK * frame, CHUNK * frame)
        return pltpu.make_async_copy(
            raw_ref.at[:, pl.ds(start, CHUNK * frame)],
            xbuf.at[:, pl.ds(start + 3 * frame, CHUNK * frame)],
            raw_sem.at[piece],
        )

    def history_copy():
        size = history.shape[1]
        last = raw_ref.at[:, pl.ds(spec * frame - size, size)]
        return remote(last, history, hist_send, hist_recv, peer(1, 0))

    barrier = pltpu.get_barrier_semaphore()
    senders = [(off, 0) for off in range(1, slabs)] + [(0, off) for off in range(1, owner_count)]
    if slabs > 1:
        senders += [(slabs - 1, off) for off in range(1, owner_count)]
    for slab, owner in senders:
        pl.semaphore_signal(barrier, inc=1, device_id=peer(slab, owner), device_id_type=MESH)

    constants = [
        pltpu.make_async_copy(src, dst, const_sem.at[n])
        for n, (src, dst) in enumerate(
            [
                (w1_any, w1_ref), (tw_any, tw_ref), (w2_any, w2_ref), (m_any, m_ref),
                (delays_any, delays_ref), (widths_any, widths_ref), (owners_any, owners_ref),
            ]
        )
    ]
    taps = [
        pltpu.make_async_copy(proto_ref.at[tap : tap + 1], proto.at[tap], proto_sem.at[tap])
        for tap in range(4)
    ]
    raw_copy(0).start()
    for copy in taps:
        copy.start()
    constants[0].start()
    constants[1].start()
    constants[2].start()
    raw_copy(1).start()
    for copy in constants[3:]:
        copy.start()
    for piece in range(2, spec // CHUNK):
        raw_copy(piece).start()
    band_ref[...] = jnp.zeros_like(band_ref)

    tile = 16 * SIDE

    def fir(ybuf, base, tiles, first=0):
        for r in tiles:
            taps = [proto[tap, :, r * tile : (r + 1) * tile].reshape(16, SIDE).astype(FT) for tap in range(4)]
            seen = []
            for k in range(-3, CHUNK):
                if first and k < 0:
                    seen.append(jnp.zeros((16, SIDE), FT))
                    continue
                start = pl.multiple_of((base + k + 3) * frame + r * tile, tile)
                seen.append(xbuf[:, pl.ds(start, tile)].reshape(16, SIDE).astype(FT))
                if k >= 0:
                    acc = (seen[k] * taps[0] + seen[k + 1] * taps[1]) + (seen[k + 2] * taps[2] + seen[k + 3] * taps[3])
                    ybuf[k // 2, r * 16 : (r + 1) * 16, k % 2 * SIDE : (k % 2 + 1) * SIDE] = acc.astype(BF16)

    def dots(ybuf, base, s, count, keep=None):
        ts = []
        for p in range(s // 2, s // 2 + count):
            a = jnp.dot(w1_ref[...], ybuf[p], preferred_element_type=F32)
            res, ims = [], []
            for m in range(2):
                re = a[:FR, m * SIDE : (m + 1) * SIDE]
                im = a[FR:, m * SIDE : (m + 1) * SIDE]
                res.append(re * tw_ref[0] - im * tw_ref[1])
                ims.append(im * tw_ref[0] + re * tw_ref[1])
            ts.append(
                jnp.concatenate(
                    [jnp.concatenate(res, 0).astype(BF16), jnp.concatenate(ims, 0).astype(BF16)], 1
                )
            )
        c = jnp.dot(jnp.concatenate(ts, 0), w2_ref[...], preferred_element_type=F32)
        re, im = c[:, :SIDE], c[:, SIDE:]
        power = re * re + im * im
        p_ref[pl.ds(pl.multiple_of((base + s) * FR, FR), 2 * count * FR)] = power
        parts = [power[k * FR : (k + 1) * FR] for k in range(2 * count)]
        if keep is not None:
            parts[:FIRST] = [jnp.where(keep, part, 0.0) for part in parts[:FIRST]]
        while len(parts) > 1:
            parts = [parts[k] + parts[k + 1] for k in range(0, len(parts), 2)]
        band_ref[...] += parts[0]

    def stage(ybuf, base, ynext, following, keep=None):
        units = CHUNK // (2 * GROUP)
        for u in range(units):
            dots(ybuf, base, 2 * GROUP * u, GROUP, keep if u == 0 else None)
            fir(ynext, following, range(8 * u // units, 8 * (u + 1) // units))

    raw_copy(0).wait()
    for copy in taps:
        copy.wait()
    fir(yone, 0, range(8), 1)
    for copy in constants[:3]:
        copy.wait()

    def chunk(step, carry):
        base = step * (2 * CHUNK)
        raw_copy(2 * step + 1).wait()

        @pl.when(step < steps - 1)
        def _():
            raw_copy(2 * step + 2).wait()

        @pl.when(step == 1)
        def _():
            pl.semaphore_wait(barrier, len(senders))
            if slabs > 1:
                history_copy().start()

        @pl.when(step == steps - 1)
        def _():
            if slabs > 1:
                history_copy().wait()
                xbuf[:, : 3 * frame] = jnp.where(tm > 0, history[...], 0.0)
            else:
                xbuf[:, : 3 * frame] = jnp.zeros((1, 3 * frame), BF16)

        stage(yone, base, ytwo, base + CHUNK, step > 0)
        following = jnp.where(step < steps - 1, base + 2 * CHUNK, 0)
        stage(ytwo, base + CHUNK, yone, following)
        return carry

    steps = spec // (2 * CHUNK)
    lax.fori_loop(0, steps, chunk, 0)
    dots(yone, 0, 0, FIRST // 2)

    copies = []
    for off in range(1, slabs):
        copy = remote(band_ref, bands.at[off - 1], band_send.at[off - 1], band_recv.at[off - 1], peer(off, 0))
        copy.start()
        copies.append(copy)

    for copy in constants[3:]:
        copy.wait()
    lanes = (MAXT + 1) * quad
    spot = iota((NBLK, SIDE), 0)
    lane = iota((NBLK, SIDE), 1) // 2
    spread = jnp.concatenate([lane == spot, lane == NBLK - 1 - spot], 1).astype(F32).astype(BF16)
    late = jnp.dot(delays_ref[...].astype(F32).astype(BF16), spread, preferred_element_type=F32)
    line = iota((quad, 2 * SIDE), 0) // trials
    masks = [
        jnp.concatenate(
            [
                jnp.where((late == float(v)) & (line == g), 1.0, 0.0)
                for v in range(MAXT + 1)
            ],
            0,
        ).astype(BF16)
        for g in range(groups)
    ]

    def column(ref):
        n = ref.shape[1]
        same = iota((n, n), 0) == iota((n, n), 1)
        return jnp.sum(jnp.where(same, jnp.broadcast_to(ref[...], (n, n)), 0), 1, keepdims=True)

    lane = iota((groups, lanes), 1) % quad
    row = iota((groups, lanes), 0)
    owner = jnp.broadcast_to(column(owners_ref), (groups, lanes))
    mine = jnp.sum(jnp.where(lane // trials == row, owner, 0), 0, keepdims=True)
    rank = jnp.sum(jnp.where((owner == mine) & (row < lane // trials), 1, 0), 0, keepdims=True)
    place = (mine * slots + rank) * trials + lane[:1] % trials
    pack = jnp.where(iota((owner_count * rows, lanes), 0) == place, 1.0, 0.0)
    pack = jnp.concatenate([pack, pack], 1).astype(BF16)

    reach = jnp.broadcast_to(column(widths_ref), (boxes, SIDE))
    root = 1.0 / jnp.sqrt(reach.astype(F32))
    root = jnp.concatenate([root] * rows, 0)
    reach = jnp.concatenate([reach] * rows, 0)
    if WMAX * rows > SIDE:
        reach = jnp.broadcast_to(reach[:, :1], (boxes * rows, WMAX * rows))
    lag = iota((boxes * rows, WMAX * rows), 1)
    series = iota((boxes * rows, WMAX * rows), 0) // boxes
    kernel = jnp.where((lag % rows == series) & (lag // rows < reach), 1.0, 0.0)
    kernel = jnp.concatenate([kernel, kernel], 1).astype(BF16)
    used = (spec + FD - 1) * groups
    direct[used:] = jnp.zeros((direct.shape[0] - used, SIDE), F32)
    mirror[used:] = jnp.zeros((direct.shape[0] - used, SIDE), F32)

    band = band_ref[...]
    for off in range(1, slabs):
        copies[off - 1].wait()
        band = band + bands[off - 1]
    scale = 1.0 / (4 * frame)
    held = iota((FR, SIDE), 0) <= HALF
    inv[...] = jnp.where(held, scale / (band * (scale / spectra) + 1e-06), 0.0)

    even = iota((FD * groups, SIDE), 1) % 2 == 0
    size = FD * groups

    def block(step, carry):
        carry = list(carry)
        for s in range(0, SPB, 2):
            flats = []
            for k in (s, s + 1):
                start = pl.multiple_of((step * SPB + k) * FR, FR)
                ratio = p_ref[pl.ds(start, FR)] * inv[...]
                total = 2.0 * jnp.sum(ratio, 0, keepdims=True) - ratio[:1] - ratio[HALF : HALF + 1]
                mean = jnp.sum(total, 1, keepdims=True) * (1.0 / frame)
                flats.append((ratio - mean).astype(BF16))
            r = jnp.dot(m_ref[...], jnp.concatenate(flats, 1), preferred_element_type=F32)
            for m in range(2):
                part = r[:, m * SIDE : (m + 1) * SIDE]
                one = jnp.where(even, part[:size], part[size : 2 * size])
                two = jnp.where(even, part[3 * size :], part[2 * size : 3 * size])
                for n, (ref, new) in enumerate(((direct, one), (mirror, two))):
                    new = [new[d * groups : (d + 1) * groups] for d in range(FD)]
                    held = carry[n * (FD - 1) : (n + 1) * (FD - 1)] + [0.0]
                    at = pl.multiple_of((step * SPB + s + m) * groups, groups)
                    ref[pl.ds(at, groups)] = held[0] + new[0]
                    for d in range(1, FD):
                        carry[n * (FD - 1) + d - 1] = held[d] + new[d]
        return tuple(carry)

    zero = jnp.zeros((groups, SIDE), F32)
    carry = lax.fori_loop(0, spec // SPB, block, (zero,) * (2 * (FD - 1)))
    for d in range(FD - 1):
        direct[(spec + d) * groups : (spec + d + 1) * groups] = carry[d]
        mirror[(spec + d) * groups : (spec + d + 1) * groups] = carry[FD - 1 + d]

    count = direct.shape[0] // groups
    each = 0.0
    for g in range(groups):
        rows_g = pl.ds(g, count, stride=groups)
        both = jnp.concatenate([direct[rows_g, :], mirror[rows_g, :]], 1).astype(BF16)
        each = each + lax.dot_general(
            both, masks[g], (((1,), (1,)), ((), ())), preferred_element_type=F32
        )
    length = count + MAXT * TT
    value = iota((length, lanes), 1) // quad
    dd = 0.0
    for v in range(MAXT + 1):
        pads = [jnp.zeros((v * TT, lanes), F32), each, jnp.zeros(((MAXT - v) * TT, lanes), F32)]
        moved = jnp.concatenate([part for part in pads if part.shape[0]], 0)
        dd = jnp.where(value == v, moved, dd)
    dd = dd * (1.0 / math.sqrt(SIDE * SIDE // NBLK) / math.sqrt(NBLK))
    back = spec - TT
    dd = jnp.concatenate([dd[:spec], dd[back:], jnp.zeros((SIDE - length + back, lanes), F32)], 0)
    high = dd.astype(BF16)
    low = (dd - high.astype(F32)).astype(BF16)
    packed = lax.dot_general(
        pack, jnp.concatenate([high, low], 1), (((1,), (1,)), ((), ())), preferred_element_type=F32
    )
    send[...] = packed[:, :spec].reshape(send.shape)
    sendb[...] = packed[:, spec:].reshape(sendb.shape)

    copies = []
    for off in range(1, owner_count):
        copy = remote(
            send.at[lax.rem(dm + off, owner_count)], got.at[dm],
            own_send.at[off - 1], own_recv.at[off - 1], peer(0, off),
        )
        copy.start()
        copies.append(copy)
    if slabs > 1:
        for off in range(owner_count):
            copy = remote(
                sendb.at[lax.rem(dm + off, owner_count)], gotb.at[dm],
                next_send.at[off], next_recv.at[off], peer(1, off),
            )
            copy.start()
            copies.append(copy)
    got[dm] = send[dm]
    for copy in copies:
        copy.wait()

    lane = iota((rows, SIDE), 1)
    stacks = []
    for d in range(owner_count):
        own = got[d]
        if slabs > 1:
            before = jnp.where(tm > 0, gotb[d], 0.0)
            own = own + jnp.where(lane < SIDE - TT, pltpu.roll(before, SIDE - TT, 1), 0.0)
            past = pltpu.roll(before, SIDE - TT, 1)
        else:
            past = jnp.zeros((rows, SIDE), F32)
        moved = [own]
        for lag in range(1, WMAX):
            moved.append(jnp.where(lane < lag, pltpu.roll(past, lag, 1), pltpu.roll(own, lag, 1)))
        stacks.append(jnp.concatenate(moved, 0))
    stack = jnp.concatenate(stacks, 1)
    high = stack.astype(BF16)
    low = (stack - high.astype(F32)).astype(BF16)
    box = jnp.dot(kernel, jnp.concatenate([high, low], 0), preferred_element_type=F32)
    for d in range(owner_count):
        done = (box[:, d * SIDE : (d + 1) * SIDE] * root).astype(BF16)
        for s in range(slots):
            out_ref[s, d] = done[s * trials * boxes : (s + 1) * trials * boxes]


def shards(axes, raw, proto, delays, widths, owners):
    taps, channels = proto.shape
    spec = raw.shape[1] // channels
    groups, trials, _ = delays.shape
    slabs, owner_count = lax.axis_size("tm"), lax.axis_size("dm")
    capacity = 2 * (groups // owner_count)
    w1, w2, tw = tables(channels)
    masks = fine_rows(groups, channels // NBLK)
    sizes = (spec * slabs, spec, groups, slabs, owner_count, axes)
    rows = -(-(spec + FD - 1) // 8) * 8
    block = pltpu.VMEM((owner_count, capacity * trials, SIDE), F32)
    sems = lambda n: pltpu.SemaphoreType.DMA((max(n, 1),))
    small = [w1, w2, tw, masks, delays.reshape(groups * trials, NBLK), widths[None], owners.T]
    out = (capacity, owner_count, trials * widths.shape[0], spec)
    box = pl.pallas_call(
        functools.partial(search_kernel, sizes),
        in_specs=[pl.BlockSpec(memory_space=pl.ANY)] * (2 + len(small)),
        out_specs=pl.BlockSpec(memory_space=pltpu.VMEM),
        out_shape=jax.ShapeDtypeStruct(out, BF16),
        scratch_shapes=[
            pltpu.VMEM((1, (spec + 3) * channels), BF16),
            pltpu.VMEM((taps, 1, channels), F32),
            *[pltpu.VMEM(value.shape, value.dtype) for value in small],
            pltpu.VMEM((CHUNK // 2, SIDE, 2 * SIDE), BF16),
            pltpu.VMEM((CHUNK // 2, SIDE, 2 * SIDE), BF16),
            pltpu.VMEM((1, 3 * channels), BF16),
            pltpu.VMEM((spec * FR, SIDE), F32),
            pltpu.VMEM((FR, SIDE), F32),
            pltpu.VMEM((max(slabs - 1, 1), FR, SIDE), F32),
            pltpu.VMEM((FR, SIDE), F32),
            pltpu.VMEM((rows * groups, SIDE), F32),
            pltpu.VMEM((rows * groups, SIDE), F32),
            block,
            block,
            block,
            block,
            sems(spec // CHUNK),
            sems(taps),
            sems(len(small)),
            pltpu.SemaphoreType.DMA,
            pltpu.SemaphoreType.DMA,
            sems(slabs - 1),
            sems(slabs - 1),
            sems(owner_count - 1),
            sems(owner_count - 1),
            sems(owner_count),
            sems(owner_count),
        ],
        compiler_params=pltpu.CompilerParams(
            vmem_limit_bytes=56 << 20, collective_id=0, has_side_effects=True
        ),
        name="search",
    )(raw, proto, *small)
    return box.reshape(capacity, owner_count, 1, trials, widths.shape[0], spec)


def solution(mesh):
    return jax.shard_map(
        functools.partial(shards, mesh.axis_names),
        mesh=mesh,
        in_specs=(P(("group", "dm", "beam"), "tm"), P(), P(), P(), P()),
        out_specs=P("dm", "group", "beam", None, None, "tm"),
        check_vma=False,
    )
```

```python
import functools
import math

import jax
import jax.numpy as jnp
import numpy as np
from jax import lax
from jax.experimental import pallas as pl
from jax.experimental.pallas import tpu as pltpu
from jax.sharding import PartitionSpec as P

SIDE = 128
NBLK = 64
FD = 4
TT = 8
MAXT = 3
WMAX = 8
SPB = 32
FIRST = 4
CHUNK = 16
GROUP = 4
AHEAD = 3
HALF = SIDE // 2
FR = 72
BACK = 128 - TT
MESH = pl.DeviceIdType.MESH
F32 = jnp.float32
BF16 = jnp.bfloat16
FT = BF16


def tables(channels):
    i = np.arange(SIDE)
    ang = (i[:, None] * i[None, :] % SIDE) * (2.0 * math.pi / SIDE)
    c, s = np.cos(ang), np.sin(ang)
    w1 = np.concatenate([c[:FR], s[:FR]], 0)
    w2 = np.block([[c, -s], [-s, -c]])
    tw = (i[:, None] * i[None, :] % channels) * (2.0 * math.pi / channels)
    twiddle = np.stack([np.cos(tw[:FR]), np.sin(tw[:FR])]).astype(np.float32)
    return jnp.asarray(w1, BF16), jnp.asarray(w2, BF16), jnp.asarray(twiddle)


def fine_rows(groups, width):
    g = np.arange(groups)[:, None]
    i = np.arange(width)[None, :]
    fine = g * FD * (width - 1 - i) // (groups * (width - 1))
    hot = np.stack([fine == step for step in range(FD)])
    hot = hot.reshape(FD, groups, width // SIDE, SIDE).transpose(2, 0, 1, 3)
    out = np.zeros((2, 2, FD, groups, FR))
    out[0, ..., : HALF + 1] = hot[..., : HALF + 1]
    out[1, ..., 1:HALF] = hot[..., : HALF : -1]
    return jnp.asarray(out.reshape(-1, FR), BF16)


def iota(shape, dim):
    return lax.broadcasted_iota(jnp.int32, shape, dim)


def search_kernel(
    sizes, raw_ref, proto_ref, w1_any, w2_any, tw_any, m_any, delays_any, widths_any, owners_any, out_ref,
    xbuf, proto, w1_ref, w2_ref, tw_ref, m_ref, delays_ref, widths_ref, owners_ref,
    yone, ytwo, history, p_ref, band_ref, bands, inv, direct, mirror, send, sendb, got, gotb,
    raw_sem, proto_sem, const_sem,
    hist_send, hist_recv, band_send, band_recv, own_send, own_recv, next_send, next_recv,
):
    spectra, spec, groups, slabs, owner_count, axes = sizes
    frame = SIDE * SIDE
    slots = out_ref.shape[0]
    boxes = widths_ref.shape[1]
    trials = out_ref.shape[2] // boxes
    quad = trials * groups
    rows = slots * trials
    tm, dm = lax.axis_index("tm"), lax.axis_index("dm")

    def peer(slab, owner):
        place = {name: lax.axis_index(name) for name in axes}
        place["tm"] = lax.rem(tm + slab, slabs)
        place["dm"] = lax.rem(dm + owner, owner_count)
        return tuple(place[name] for name in axes)

    def remote(src, dst, send_sem, recv_sem, target):
        return pltpu.make_async_remote_copy(
            src_ref=src, dst_ref=dst, send_sem=send_sem, recv_sem=recv_sem,
            device_id=target, device_id_type=MESH,
        )

    def raw_copy(piece):
        start = pl.multiple_of(piece * CHUNK * frame, CHUNK * frame)
        return pltpu.make_async_copy(
            raw_ref.at[:, pl.ds(start, CHUNK * frame)],
            xbuf.at[:, pl.ds(start + 3 * frame, CHUNK * frame)],
            raw_sem.at[piece],
        )

    def history_copy():
        size = history.shape[1]
        last = raw_ref.at[:, pl.ds(spec * frame - size, size)]
        return remote(last, history, hist_send, hist_recv, peer(1, 0))

    barrier = pltpu.get_barrier_semaphore()
    senders = [(off, 0) for off in range(1, slabs)] + [(0, off) for off in range(1, owner_count)]
    if slabs > 1:
        senders += [(slabs - 1, off) for off in range(1, owner_count)]
    for slab, owner in senders:
        pl.semaphore_signal(barrier, inc=1, device_id=peer(slab, owner), device_id_type=MESH)

    constants = [
        pltpu.make_async_copy(src, dst, const_sem.at[n])
        for n, (src, dst) in enumerate(
            [
                (w1_any, w1_ref), (tw_any, tw_ref), (w2_any, w2_ref), (m_any, m_ref),
                (delays_any, delays_ref), (widths_any, widths_ref), (owners_any, owners_ref),
            ]
        )
    ]
    taps = [
        pltpu.make_async_copy(proto_ref.at[tap : tap + 1], proto.at[tap], proto_sem.at[tap])
        for tap in range(4)
    ]
    raw_copy(0).start()
    for copy in taps:
        copy.start()
    constants[0].start()
    constants[1].start()
    constants[2].start()
    raw_copy(1).start()
    for copy in constants[3:]:
        copy.start()
    for piece in range(2, AHEAD):
        raw_copy(piece).start()
    band_ref[...] = jnp.zeros_like(band_ref)

    tile = 16 * SIDE

    def fir(ybuf, base, tiles, first=0):
        for r in tiles:
            taps = [proto[tap, :, r * tile : (r + 1) * tile].reshape(16, SIDE).astype(FT) for tap in range(4)]
            seen = []
            for k in range(-3, CHUNK):
                if first and k < 0:
                    seen.append(jnp.zeros((16, SIDE), FT))
                    continue
                start = pl.multiple_of((base + k + 3) * frame + r * tile, tile)
                seen.append(xbuf[:, pl.ds(start, tile)].reshape(16, SIDE).astype(FT))
                if k >= 0:
                    acc = (seen[k] * taps[0] + seen[k + 1] * taps[1]) + (seen[k + 2] * taps[2] + seen[k + 3] * taps[3])
                    ybuf[k // 2, r * 16 : (r + 1) * 16, k % 2 * SIDE : (k % 2 + 1) * SIDE] = acc.astype(BF16)

    def dots(ybuf, base, s, count, keep=None):
        ts = []
        for p in range(s // 2, s // 2 + count):
            a = jnp.dot(w1_ref[...], ybuf[p], preferred_element_type=F32)
            res, ims = [], []
            for m in range(2):
                re = a[:FR, m * SIDE : (m + 1) * SIDE]
                im = a[FR:, m * SIDE : (m + 1) * SIDE]
                res.append(re * tw_ref[0] - im * tw_ref[1])
                ims.append(im * tw_ref[0] + re * tw_ref[1])
            ts.append(
                jnp.concatenate(
                    [jnp.concatenate(res, 0).astype(BF16), jnp.concatenate(ims, 0).astype(BF16)], 1
                )
            )
        c = jnp.dot(jnp.concatenate(ts, 0), w2_ref[...], preferred_element_type=F32)
        re, im = c[:, :SIDE], c[:, SIDE:]
        power = re * re + im * im
        p_ref[pl.ds(pl.multiple_of((base + s) * FR, FR), 2 * count * FR)] = power
        parts = [power[k * FR : (k + 1) * FR] for k in range(2 * count)]
        if keep is not None:
            parts[:FIRST] = [jnp.where(keep, part, 0.0) for part in parts[:FIRST]]
        while len(parts) > 1:
            parts = [parts[k] + parts[k + 1] for k in range(0, len(parts), 2)]
        band_ref[...] += parts[0]

    def stage(ybuf, base, ynext, following, keep=None):
        units = CHUNK // (2 * GROUP)
        for u in range(units):
            dots(ybuf, base, 2 * GROUP * u, GROUP, keep if u == 0 else None)
            fir(ynext, following, range(8 * u // units, 8 * (u + 1) // units))

    pl.semaphore_wait(barrier, len(senders))
    if slabs > 1:
        history_copy().start()
    raw_copy(0).wait()
    for copy in taps:
        copy.wait()
    raw_copy(AHEAD).start()
    fir(yone, 0, range(8), 1)
    for copy in constants[:3]:
        copy.wait()

    def chunk(step, carry):
        base = step * (2 * CHUNK)

        def arrive(piece):
            @pl.when(piece < pieces)
            def _():
                raw_copy(piece).wait()

            @pl.when(piece + AHEAD < pieces)
            def _():
                raw_copy(piece + AHEAD).start()

        arrive(2 * step + 1)

        stage(yone, base, ytwo, base + CHUNK, step > 0)
        arrive(2 * step + 2)

        @pl.when(step == steps - 1)
        def _():
            if slabs > 1:
                history_copy().wait()
                xbuf[:, : 3 * frame] = jnp.where(tm > 0, history[...], 0.0)
            else:
                xbuf[:, : 3 * frame] = jnp.zeros((1, 3 * frame), BF16)

        following = jnp.where(step < steps - 1, base + 2 * CHUNK, 0)
        stage(ytwo, base + CHUNK, yone, following)
        return carry

    pieces = spec // CHUNK
    steps = pieces // 2
    lax.fori_loop(0, steps, chunk, 0)
    dots(yone, 0, 0, FIRST // 2)

    copies = []
    for off in range(1, slabs):
        copy = remote(band_ref, bands.at[off - 1], band_send.at[off - 1], band_recv.at[off - 1], peer(off, 0))
        copy.start()
        copies.append(copy)

    for copy in constants[3:]:
        copy.wait()
    lanes = (MAXT + 1) * quad
    spot = iota((NBLK, SIDE), 0)
    lane = iota((NBLK, SIDE), 1) // 2
    spread = jnp.concatenate([lane == spot, lane == NBLK - 1 - spot], 1).astype(F32).astype(BF16)
    late = jnp.dot(delays_ref[...].astype(F32).astype(BF16), spread, preferred_element_type=F32)
    line = iota((quad, 2 * SIDE), 0) // trials
    masks = [
        jnp.concatenate(
            [
                jnp.where((late == float(v)) & (line == g), 1.0, 0.0)
                for v in range(MAXT + 1)
            ],
            0,
        ).astype(BF16)
        for g in range(groups)
    ]

    def column(ref):
        n = ref.shape[1]
        same = iota((n, n), 0) == iota((n, n), 1)
        return jnp.sum(jnp.where(same, jnp.broadcast_to(ref[...], (n, n)), 0), 1, keepdims=True)

    lane = iota((groups, lanes), 1) % quad
    row = iota((groups, lanes), 0)
    owner = jnp.broadcast_to(column(owners_ref), (groups, lanes))
    mine = jnp.sum(jnp.where(lane // trials == row, owner, 0), 0, keepdims=True)
    rank = jnp.sum(jnp.where((owner == mine) & (row < lane // trials), 1, 0), 0, keepdims=True)
    place = (mine * slots + rank) * trials + lane[:1] % trials
    pack = jnp.where(iota((owner_count * rows, lanes), 0) == place, 1.0, 0.0)
    pack = jnp.concatenate([pack, pack], 1).astype(BF16)

    reach = jnp.broadcast_to(column(widths_ref), (boxes, SIDE))
    root = 1.0 / jnp.sqrt(reach.astype(F32))
    root = jnp.concatenate([root] * rows, 0)
    reach = jnp.concatenate([reach] * rows, 0)
    if WMAX * rows > SIDE:
        reach = jnp.broadcast_to(reach[:, :1], (boxes * rows, WMAX * rows))
    lag = iota((boxes * rows, WMAX * rows), 1)
    series = iota((boxes * rows, WMAX * rows), 0) // boxes
    kernel = jnp.where((lag % rows == series) & (lag // rows < reach), 1.0, 0.0)
    kernel = jnp.concatenate([kernel, kernel], 1).astype(BF16)
    used = (spec + FD - 1) * groups
    direct[used:] = jnp.zeros((direct.shape[0] - used, SIDE), F32)
    mirror[used:] = jnp.zeros((direct.shape[0] - used, SIDE), F32)

    band = band_ref[...]
    for off in range(1, slabs):
        copies[off - 1].wait()
        band = band + bands[off - 1]
    scale = 1.0 / (4 * frame)
    held = iota((FR, SIDE), 0) <= HALF
    inv[...] = jnp.where(held, scale / (band * (scale / spectra) + 1e-06), 0.0)

    even = iota((FD * groups, SIDE), 1) % 2 == 0
    size = FD * groups

    def block(step, carry):
        carry = list(carry)
        for s in range(0, SPB, 2):
            flats = []
            for k in (s, s + 1):
                start = pl.multiple_of((step * SPB + k) * FR, FR)
                ratio = p_ref[pl.ds(start, FR)] * inv[...]
                total = 2.0 * jnp.sum(ratio, 0, keepdims=True) - ratio[:1] - ratio[HALF : HALF + 1]
                mean = jnp.sum(total, 1, keepdims=True) * (1.0 / frame)
                flats.append((ratio - mean).astype(BF16))
            r = jnp.dot(m_ref[...], jnp.concatenate(flats, 1), preferred_element_type=F32)
            for m in range(2):
                part = r[:, m * SIDE : (m + 1) * SIDE]
                one = jnp.where(even, part[:size], part[size : 2 * size])
                two = jnp.where(even, part[3 * size :], part[2 * size : 3 * size])
                for n, (ref, new) in enumerate(((direct, one), (mirror, two))):
                    new = [new[d * groups : (d + 1) * groups] for d in range(FD)]
                    held = carry[n * (FD - 1) : (n + 1) * (FD - 1)] + [0.0]
                    at = pl.multiple_of((step * SPB + s + m) * groups, groups)
                    ref[pl.ds(at, groups)] = held[0] + new[0]
                    for d in range(1, FD):
                        carry[n * (FD - 1) + d - 1] = held[d] + new[d]
        return tuple(carry)

    zero = jnp.zeros((groups, SIDE), F32)
    carry = lax.fori_loop(0, spec // SPB, block, (zero,) * (2 * (FD - 1)))
    for d in range(FD - 1):
        direct[(spec + d) * groups : (spec + d + 1) * groups] = carry[d]
        mirror[(spec + d) * groups : (spec + d + 1) * groups] = carry[FD - 1 + d]

    count = direct.shape[0] // groups
    each = 0.0
    for g in range(groups):
        rows_g = pl.ds(g, count, stride=groups)
        both = jnp.concatenate([direct[rows_g, :], mirror[rows_g, :]], 1).astype(BF16)
        each = each + lax.dot_general(
            both, masks[g], (((1,), (1,)), ((), ())), preferred_element_type=F32
        )
    length = count + MAXT * TT
    value = iota((length, lanes), 1) // quad
    dd = 0.0
    for v in range(MAXT + 1):
        pads = [jnp.zeros((v * TT, lanes), F32), each, jnp.zeros(((MAXT - v) * TT, lanes), F32)]
        moved = jnp.concatenate([part for part in pads if part.shape[0]], 0)
        dd = jnp.where(value == v, moved, dd)
    dd = dd * (1.0 / math.sqrt(SIDE * SIDE // NBLK) / math.sqrt(NBLK))
    back = spec - TT
    dd = jnp.concatenate([dd[:spec], dd[back:], jnp.zeros((SIDE - length + back, lanes), F32)], 0)
    high = dd.astype(BF16)
    low = (dd - high.astype(F32)).astype(BF16)
    packed = lax.dot_general(
        pack, jnp.concatenate([high, low], 1), (((1,), (1,)), ((), ())), preferred_element_type=F32
    )
    send[...] = packed[:, :spec].reshape(send.shape)
    sendb[...] = packed[:, spec:].reshape(sendb.shape)

    copies = []
    for off in range(1, owner_count):
        copy = remote(
            send.at[lax.rem(dm + off, owner_count)], got.at[dm],
            own_send.at[off - 1], own_recv.at[off - 1], peer(0, off),
        )
        copy.start()
        copies.append(copy)
    if slabs > 1:
        for off in range(owner_count):
            copy = remote(
                sendb.at[lax.rem(dm + off, owner_count)], gotb.at[dm],
                next_send.at[off], next_recv.at[off], peer(1, off),
            )
            copy.start()
            copies.append(copy)
    got[dm] = send[dm]
    for copy in copies:
        copy.wait()

    lane = iota((rows, SIDE), 1)
    stacks = []
    for d in range(owner_count):
        own = got[d]
        if slabs > 1:
            before = jnp.where(tm > 0, gotb[d], 0.0)
            own = own + jnp.where(lane < SIDE - TT, pltpu.roll(before, SIDE - TT, 1), 0.0)
            past = pltpu.roll(before, SIDE - TT, 1)
        else:
            past = jnp.zeros((rows, SIDE), F32)
        moved = [own]
        for lag in range(1, WMAX):
            moved.append(jnp.where(lane < lag, pltpu.roll(past, lag, 1), pltpu.roll(own, lag, 1)))
        stacks.append(jnp.concatenate(moved, 0))
    stack = jnp.concatenate(stacks, 1)
    high = stack.astype(BF16)
    low = (stack - high.astype(F32)).astype(BF16)
    box = jnp.dot(kernel, jnp.concatenate([high, low], 0), preferred_element_type=F32)
    for d in range(owner_count):
        done = (box[:, d * SIDE : (d + 1) * SIDE] * root).astype(BF16)
        for s in range(slots):
            out_ref[s, d] = done[s * trials * boxes : (s + 1) * trials * boxes]


def shards(axes, raw, proto, delays, widths, owners):
    taps, channels = proto.shape
    spec = raw.shape[1] // channels
    groups, trials, _ = delays.shape
    slabs, owner_count = lax.axis_size("tm"), lax.axis_size("dm")
    capacity = 2 * (groups // owner_count)
    w1, w2, tw = tables(channels)
    masks = fine_rows(groups, channels // NBLK)
    sizes = (spec * slabs, spec, groups, slabs, owner_count, axes)
    rows = -(-(spec + FD - 1) // 8) * 8
    block = pltpu.VMEM((owner_count, capacity * trials, SIDE), F32)
    sems = lambda n: pltpu.SemaphoreType.DMA((max(n, 1),))
    small = [w1, w2, tw, masks, delays.reshape(groups * trials, NBLK), widths[None], owners.T]
    out = (capacity, owner_count, trials * widths.shape[0], spec)
    box = pl.pallas_call(
        functools.partial(search_kernel, sizes),
        in_specs=[pl.BlockSpec(memory_space=pl.ANY)] * (2 + len(small)),
        out_specs=pl.BlockSpec(memory_space=pltpu.VMEM),
        out_shape=pltpu.VMEM(out, BF16),
        scratch_shapes=[
            pltpu.VMEM((1, (spec + 3) * channels), BF16),
            pltpu.VMEM((taps, 1, channels), F32),
            *[pltpu.VMEM(value.shape, value.dtype) for value in small],
            pltpu.VMEM((CHUNK // 2, SIDE, 2 * SIDE), BF16),
            pltpu.VMEM((CHUNK // 2, SIDE, 2 * SIDE), BF16),
            pltpu.VMEM((1, 3 * channels), BF16),
            pltpu.VMEM((spec * FR, SIDE), F32),
            pltpu.VMEM((FR, SIDE), F32),
            pltpu.VMEM((max(slabs - 1, 1), FR, SIDE), F32),
            pltpu.VMEM((FR, SIDE), F32),
            pltpu.VMEM((rows * groups, SIDE), F32),
            pltpu.VMEM((rows * groups, SIDE), F32),
            block,
            block,
            block,
            block,
            sems(spec // CHUNK),
            sems(taps),
            sems(len(small)),
            pltpu.SemaphoreType.DMA,
            pltpu.SemaphoreType.DMA,
            sems(slabs - 1),
            sems(slabs - 1),
            sems(owner_count - 1),
            sems(owner_count - 1),
            sems(owner_count),
            sems(owner_count),
        ],
        compiler_params=pltpu.CompilerParams(
            vmem_limit_bytes=56 << 20, collective_id=0, has_side_effects=True
        ),
        name="search",
    )(raw, proto, *small)
    return box.reshape(capacity, owner_count, 1, trials, widths.shape[0], spec)


def solution(mesh):
    return jax.shard_map(
        functools.partial(shards, mesh.axis_names),
        mesh=mesh,
        in_specs=(P(("group", "dm", "beam"), "tm"), P(), P(), P(), P()),
        out_specs=P("dm", "group", "beam", None, None, "tm"),
        check_vma=False,
    )
```

```python
import functools
import math

import jax
import jax.numpy as jnp
import numpy as np
from jax import lax
from jax.experimental import pallas as pl
from jax.experimental.pallas import tpu as pltpu
from jax.sharding import PartitionSpec as P

SIDE = 128
NBLK = 64
FD = 4
TT = 8
MAXT = 3
WMAX = 8
SPB = 64
FIRST = 4
CHUNK = 16
GROUP = 4
AHEAD = 3
HALF = SIDE // 2
FR = 72
BACK = 128 - TT
MESH = pl.DeviceIdType.MESH
F32 = jnp.float32
BF16 = jnp.bfloat16
FT = BF16


def tables(channels):
    i = np.arange(SIDE)
    ang = (i[:, None] * i[None, :] % SIDE) * (2.0 * math.pi / SIDE)
    c, s = np.cos(ang), np.sin(ang)
    w1 = np.concatenate([c[:FR], s[:FR]], 0)
    w2 = np.block([[c, -s], [-s, -c]])
    tw = (i[:, None] * i[None, :] % channels) * (2.0 * math.pi / channels)
    twiddle = np.stack([np.cos(tw[:FR]), np.sin(tw[:FR])]).astype(np.float32)
    return jnp.asarray(w1, BF16), jnp.asarray(w2, BF16), jnp.asarray(twiddle)


def fine_rows(groups, width):
    g = np.arange(groups)[:, None]
    i = np.arange(width)[None, :]
    fine = g * FD * (width - 1 - i) // (groups * (width - 1))
    hot = np.stack([fine == step for step in range(FD)])
    hot = hot.reshape(FD, groups, width // SIDE, SIDE).transpose(2, 0, 1, 3)
    out = np.zeros((2, 2, FD, groups, FR))
    out[0, ..., : HALF + 1] = hot[..., : HALF + 1]
    out[1, ..., 1:HALF] = hot[..., : HALF : -1]
    return jnp.asarray(out.reshape(-1, FR), BF16)


def iota(shape, dim):
    return lax.broadcasted_iota(jnp.int32, shape, dim)


def search_kernel(
    sizes, raw_ref, proto_ref, w1_any, w2_any, tw_any, m_any, delays_any, widths_any, owners_any, out_ref,
    xbuf, proto, w1_ref, w2_ref, tw_ref, m_ref, delays_ref, widths_ref, owners_ref,
    yone, ytwo, history, p_ref, band_ref, bands, inv, direct, mirror, send, sendb, got, gotb,
    raw_sem, proto_sem, const_sem,
    hist_send, hist_recv, band_send, band_recv, own_send, own_recv, next_send, next_recv,
):
    spectra, spec, groups, slabs, owner_count, axes = sizes
    frame = SIDE * SIDE
    slots = out_ref.shape[0]
    boxes = widths_ref.shape[1]
    trials = out_ref.shape[2] // boxes
    quad = trials * groups
    rows = slots * trials
    tm, dm = lax.axis_index("tm"), lax.axis_index("dm")

    def peer(slab, owner):
        place = {name: lax.axis_index(name) for name in axes}
        place["tm"] = lax.rem(tm + slab, slabs)
        place["dm"] = lax.rem(dm + owner, owner_count)
        return tuple(place[name] for name in axes)

    def remote(src, dst, send_sem, recv_sem, target):
        return pltpu.make_async_remote_copy(
            src_ref=src, dst_ref=dst, send_sem=send_sem, recv_sem=recv_sem,
            device_id=target, device_id_type=MESH,
        )

    def raw_copy(piece):
        start = pl.multiple_of(piece * CHUNK * frame, CHUNK * frame)
        return pltpu.make_async_copy(
            raw_ref.at[:, pl.ds(start, CHUNK * frame)],
            xbuf.at[:, pl.ds(start + 3 * frame, CHUNK * frame)],
            raw_sem.at[piece],
        )

    def history_copy():
        size = history.shape[1]
        last = raw_ref.at[:, pl.ds(spec * frame - size, size)]
        return remote(last, history, hist_send, hist_recv, peer(1, 0))

    barrier = pltpu.get_barrier_semaphore()
    senders = [(off, 0) for off in range(1, slabs)] + [(0, off) for off in range(1, owner_count)]
    if slabs > 1:
        senders += [(slabs - 1, off) for off in range(1, owner_count)]
    for slab, owner in senders:
        pl.semaphore_signal(barrier, inc=1, device_id=peer(slab, owner), device_id_type=MESH)

    constants = [
        pltpu.make_async_copy(src, dst, const_sem.at[n])
        for n, (src, dst) in enumerate(
            [
                (w1_any, w1_ref), (tw_any, tw_ref), (w2_any, w2_ref), (m_any, m_ref),
                (delays_any, delays_ref), (widths_any, widths_ref), (owners_any, owners_ref),
            ]
        )
    ]
    taps = [
        pltpu.make_async_copy(proto_ref.at[tap : tap + 1], proto.at[tap], proto_sem.at[tap])
        for tap in range(4)
    ]
    raw_copy(0).start()
    for copy in taps:
        copy.start()
    constants[0].start()
    constants[1].start()
    constants[2].start()
    raw_copy(1).start()
    for copy in constants[3:]:
        copy.start()
    for piece in range(2, AHEAD):
        raw_copy(piece).start()
    band_ref[...] = jnp.zeros_like(band_ref)
    xbuf[:, : 3 * frame] = jnp.zeros((1, 3 * frame), BF16)

    tile = 16 * SIDE

    def fir(ybuf, base, tiles, count=CHUNK):
        for r in tiles:
            taps = [proto[tap, :, r * tile : (r + 1) * tile].reshape(16, SIDE).astype(FT) for tap in range(4)]
            seen = []
            for k in range(-3, count):
                start = pl.multiple_of((base + k + 3) * frame + r * tile, tile)
                seen.append(xbuf[:, pl.ds(start, tile)].reshape(16, SIDE).astype(FT))
                if k >= 0:
                    acc = (seen[k] * taps[0] + seen[k + 1] * taps[1]) + (seen[k + 2] * taps[2] + seen[k + 3] * taps[3])
                    ybuf[k // 2, r * 16 : (r + 1) * 16, k % 2 * SIDE : (k % 2 + 1) * SIDE] = acc.astype(BF16)

    def dots(ybuf, base, s, count, keep=None):
        ts = []
        for p in range(s // 2, s // 2 + count):
            a = jnp.dot(w1_ref[...], ybuf[p], preferred_element_type=F32)
            res, ims = [], []
            for m in range(2):
                re = a[:FR, m * SIDE : (m + 1) * SIDE]
                im = a[FR:, m * SIDE : (m + 1) * SIDE]
                res.append(re * tw_ref[0] - im * tw_ref[1])
                ims.append(im * tw_ref[0] + re * tw_ref[1])
            ts.append(
                jnp.concatenate(
                    [jnp.concatenate(res, 0).astype(BF16), jnp.concatenate(ims, 0).astype(BF16)], 1
                )
            )
        c = jnp.dot(jnp.concatenate(ts, 0), w2_ref[...], preferred_element_type=F32)
        re, im = c[:, :SIDE], c[:, SIDE:]
        power = re * re + im * im
        p_ref[pl.ds(pl.multiple_of((base + s) * FR, FR), 2 * count * FR)] = power
        parts = [power[k * FR : (k + 1) * FR] for k in range(2 * count)]
        if keep is not None:
            parts[:FIRST] = [jnp.where(keep, part, 0.0) for part in parts[:FIRST]]
        while len(parts) > 1:
            parts = [parts[k] + parts[k + 1] for k in range(0, len(parts), 2)]
        band_ref[...] += parts[0]

    def stage(ybuf, base, ynext, following, keep=None):
        units = CHUNK // (2 * GROUP)
        for u in range(units):
            dots(ybuf, base, 2 * GROUP * u, GROUP, keep if u == 0 else None)
            fir(ynext, following, range(8 * u // units, 8 * (u + 1) // units))

    pl.semaphore_wait(barrier, len(senders))
    if slabs > 1:
        history_copy().start()
    raw_copy(0).wait()
    for copy in taps:
        copy.wait()
    raw_copy(AHEAD).start()
    fir(yone, 0, range(8))
    for copy in constants[:3]:
        copy.wait()

    def chunk(step, carry):
        base = step * (2 * CHUNK)

        def arrive(piece):
            @pl.when(piece < pieces)
            def _():
                raw_copy(piece).wait()

            @pl.when(piece + AHEAD < pieces)
            def _():
                raw_copy(piece + AHEAD).start()

        arrive(2 * step + 1)
        arrive(2 * step + 2)

        stage(yone, base, ytwo, base + CHUNK, step > 0)
        following = jnp.where(step < steps - 1, base + 2 * CHUNK, 0)
        stage(ytwo, base + CHUNK, yone, following)
        return carry

    pieces = spec // CHUNK
    steps = pieces // 2
    lax.fori_loop(0, steps, chunk, 0)
    if slabs > 1:
        history_copy().wait()
        xbuf[:, : 3 * frame] = jnp.where(tm > 0, history[...], 0.0)
        fir(yone, 0, range(8), FIRST)
    dots(yone, 0, 0, FIRST // 2)

    copies = []
    for off in range(1, slabs):
        copy = remote(band_ref, bands.at[off - 1], band_send.at[off - 1], band_recv.at[off - 1], peer(off, 0))
        copy.start()
        copies.append(copy)

    for copy in constants[3:]:
        copy.wait()
    lanes = (MAXT + 1) * quad
    spot = iota((NBLK, SIDE), 0)
    lane = iota((NBLK, SIDE), 1) // 2
    spread = jnp.concatenate([lane == spot, lane == NBLK - 1 - spot], 1).astype(F32).astype(BF16)
    late = jnp.dot(delays_ref[...].astype(F32).astype(BF16), spread, preferred_element_type=F32)
    line = iota((quad, 2 * SIDE), 0) // trials
    masks = [
        jnp.concatenate(
            [
                jnp.where((late == float(v)) & (line == g), 1.0, 0.0)
                for v in range(MAXT + 1)
            ],
            0,
        ).astype(BF16)
        for g in range(groups)
    ]

    def column(ref):
        n = ref.shape[1]
        same = iota((n, n), 0) == iota((n, n), 1)
        return jnp.sum(jnp.where(same, jnp.broadcast_to(ref[...], (n, n)), 0), 1, keepdims=True)

    lane = iota((groups, lanes), 1) % quad
    row = iota((groups, lanes), 0)
    owner = jnp.broadcast_to(column(owners_ref), (groups, lanes))
    mine = jnp.sum(jnp.where(lane // trials == row, owner, 0), 0, keepdims=True)
    rank = jnp.sum(jnp.where((owner == mine) & (row < lane // trials), 1, 0), 0, keepdims=True)
    place = (mine * slots + rank) * trials + lane[:1] % trials
    pack = jnp.where(iota((owner_count * rows, lanes), 0) == place, 1.0, 0.0)
    pack = jnp.concatenate([pack, pack], 1).astype(BF16)

    reach = jnp.broadcast_to(column(widths_ref), (boxes, SIDE))
    root = 1.0 / jnp.sqrt(reach.astype(F32))
    root = jnp.concatenate([root] * rows, 0)
    reach = jnp.concatenate([reach] * rows, 0)
    if WMAX * rows > SIDE:
        reach = jnp.broadcast_to(reach[:, :1], (boxes * rows, WMAX * rows))
    lag = iota((boxes * rows, WMAX * rows), 1)
    series = iota((boxes * rows, WMAX * rows), 0) // boxes
    kernel = jnp.where((lag % rows == series) & (lag // rows < reach), 1.0, 0.0)
    kernel = jnp.concatenate([kernel, kernel], 1).astype(BF16)
    used = (spec + FD - 1) * groups
    direct[used:] = jnp.zeros((direct.shape[0] - used, SIDE), F32)
    mirror[used:] = jnp.zeros((direct.shape[0] - used, SIDE), F32)

    band = band_ref[...]
    for off in range(1, slabs):
        copies[off - 1].wait()
        band = band + bands[off - 1]
    scale = 1.0 / (4 * frame)
    held = iota((FR, SIDE), 0) <= HALF
    inv[...] = jnp.where(held, scale / (band * (scale / spectra) + 1e-06), 0.0)

    even = iota((FD * groups, SIDE), 1) % 2 == 0
    size = FD * groups

    def flat(step, k):
        ratio = p_ref[pl.ds(pl.multiple_of((step * SPB + k) * FR, FR), FR)] * inv[...]
        total = 2.0 * jnp.sum(ratio, 0, keepdims=True) - ratio[:1] - ratio[HALF : HALF + 1]
        mean = jnp.sum(total, 1, keepdims=True) * (1.0 / frame)
        return (ratio - mean).astype(BF16)

    def block(step, carry):
        carry = list(carry)
        for s in range(0, SPB, 2):
            flats = jnp.concatenate([flat(step, s), flat(step, s + 1)], 1)
            r = jnp.dot(m_ref[...], flats, preferred_element_type=F32)
            for m in range(2):
                part = r[:, m * SIDE : (m + 1) * SIDE]
                one = jnp.where(even, part[:size], part[size : 2 * size])
                two = jnp.where(even, part[3 * size :], part[2 * size : 3 * size])
                for n, (ref, new) in enumerate(((direct, one), (mirror, two))):
                    new = [new[d * groups : (d + 1) * groups] for d in range(FD)]
                    held = carry[n * (FD - 1) : (n + 1) * (FD - 1)] + [0.0]
                    at = pl.multiple_of((step * SPB + s + m) * groups, groups)
                    ref[pl.ds(at, groups)] = held[0] + new[0]
                    for d in range(1, FD):
                        carry[n * (FD - 1) + d - 1] = held[d] + new[d]
        return tuple(carry)

    def sweep(first, last):
        zero = jnp.zeros((groups, SIDE), F32)
        return lax.fori_loop(first, last, block, (zero,) * (2 * (FD - 1)))

    def series(first, count):
        each = 0.0
        for g in range(groups):
            picked = pl.ds(first * groups + g, count, stride=groups)
            both = jnp.concatenate([direct[picked, :], mirror[picked, :]], 1).astype(BF16)
            each = each + lax.dot_general(
                both, masks[g], (((1,), (1,)), ((), ())), preferred_element_type=F32
            )
        return each * (1.0 / math.sqrt(SIDE * SIDE // NBLK) / math.sqrt(NBLK))

    def gather(each, skip, count):
        length = skip + count
        padded = each
        if length > each.shape[0]:
            padded = jnp.concatenate([each, jnp.zeros((length - each.shape[0], lanes), F32)], 0)
        value = iota((count, lanes), 1) // quad
        dd = 0.0
        for v in range(MAXT + 1):
            start = skip - v * TT
            if start < 0:
                moved = jnp.concatenate([jnp.zeros((-start, lanes), F32), padded[: count + start]], 0)
            else:
                moved = padded[start : start + count]
            dd = jnp.where(value == v, moved, dd)
        if count < SIDE:
            dd = jnp.concatenate([dd, jnp.zeros((SIDE - count, lanes), F32)], 0)
        high = dd.astype(BF16)
        low = (dd - high.astype(F32)).astype(BF16)
        return lax.dot_general(
            pack, jnp.concatenate([high, low], 1), (((1,), (1,)), ((), ())), preferred_element_type=F32
        )

    blocks = spec // SPB
    middle = blocks // 2
    count = direct.shape[0] // groups
    carry = sweep(middle, blocks)
    for d in range(FD - 1):
        direct[(spec + d) * groups : (spec + d + 1) * groups] = carry[d]
        mirror[(spec + d) * groups : (spec + d + 1) * groups] = carry[FD - 1 + d]
    copies = []
    if slabs > 1:
        reach = (MAXT + 1) * TT
        late = series(spec - reach, count - spec + reach)
        sendb[...] = gather(late, reach - TT, count - spec + reach).reshape(sendb.shape)
        for off in range(owner_count - 1, -1, -1):
            copy = remote(
                sendb.at[lax.rem(dm + off, owner_count)], gotb.at[dm],
                next_send.at[off], next_recv.at[off], peer(1, off),
            )
            copy.start()
            copies.append(copy)
    carry = sweep(0, middle)
    for d in range(FD - 1):
        start = (middle * SPB + d) * groups
        direct[start : start + groups] += carry[d]
        mirror[start : start + groups] += carry[FD - 1 + d]
    send[...] = gather(series(0, spec), 0, spec).reshape(send.shape)
    for off in range(1, owner_count):
        copy = remote(
            send.at[lax.rem(dm + off, owner_count)], got.at[dm],
            own_send.at[off - 1], own_recv.at[off - 1], peer(0, off),
        )
        copy.start()
        copies.append(copy)
    got[dm] = send[dm]
    for copy in copies:
        copy.wait()

    lane = iota((rows, SIDE), 1)
    stacks = []
    for d in range(owner_count):
        own = got[d]
        if slabs > 1:
            before = jnp.where(tm > 0, gotb[d], 0.0)
            own = own + jnp.where(lane < SIDE - TT, pltpu.roll(before, SIDE - TT, 1), 0.0)
            past = pltpu.roll(before, SIDE - TT, 1)
        else:
            past = jnp.zeros((rows, SIDE), F32)
        moved = [own]
        for lag in range(1, WMAX):
            moved.append(jnp.where(lane < lag, pltpu.roll(past, lag, 1), pltpu.roll(own, lag, 1)))
        stacks.append(jnp.concatenate(moved, 0))
    stack = jnp.concatenate(stacks, 1)
    high = stack.astype(BF16)
    low = (stack - high.astype(F32)).astype(BF16)
    box = jnp.dot(kernel, jnp.concatenate([high, low], 0), preferred_element_type=F32)
    for d in range(owner_count):
        done = (box[:, d * SIDE : (d + 1) * SIDE] * root).astype(BF16)
        for s in range(slots):
            out_ref[s, d] = done[s * trials * boxes : (s + 1) * trials * boxes]


def shards(axes, raw, proto, delays, widths, owners):
    taps, channels = proto.shape
    spec = raw.shape[1] // channels
    groups, trials, _ = delays.shape
    slabs, owner_count = lax.axis_size("tm"), lax.axis_size("dm")
    capacity = 2 * (groups // owner_count)
    w1, w2, tw = tables(channels)
    masks = fine_rows(groups, channels // NBLK)
    sizes = (spec * slabs, spec, groups, slabs, owner_count, axes)
    rows = -(-(spec + FD - 1) // 8) * 8
    block = pltpu.VMEM((owner_count, capacity * trials, SIDE), F32)
    sems = lambda n: pltpu.SemaphoreType.DMA((max(n, 1),))
    small = [w1, w2, tw, masks, delays.reshape(groups * trials, NBLK), widths[None], owners.T]
    out = (capacity, owner_count, trials * widths.shape[0], spec)
    box = pl.pallas_call(
        functools.partial(search_kernel, sizes),
        in_specs=[pl.BlockSpec(memory_space=pl.ANY)] * (2 + len(small)),
        out_specs=pl.BlockSpec(memory_space=pltpu.VMEM),
        out_shape=pltpu.VMEM(out, BF16),
        scratch_shapes=[
            pltpu.VMEM((1, (spec + 3) * channels), BF16),
            pltpu.VMEM((taps, 1, channels), F32),
            *[pltpu.VMEM(value.shape, value.dtype) for value in small],
            pltpu.VMEM((CHUNK // 2, SIDE, 2 * SIDE), BF16),
            pltpu.VMEM((CHUNK // 2, SIDE, 2 * SIDE), BF16),
            pltpu.VMEM((1, 3 * channels), BF16),
            pltpu.VMEM((spec * FR, SIDE), F32),
            pltpu.VMEM((FR, SIDE), F32),
            pltpu.VMEM((max(slabs - 1, 1), FR, SIDE), F32),
            pltpu.VMEM((FR, SIDE), F32),
            pltpu.VMEM((rows * groups, SIDE), F32),
            pltpu.VMEM((rows * groups, SIDE), F32),
            block,
            block,
            block,
            block,
            sems(spec // CHUNK),
            sems(taps),
            sems(len(small)),
            pltpu.SemaphoreType.DMA,
            pltpu.SemaphoreType.DMA,
            sems(slabs - 1),
            sems(slabs - 1),
            sems(owner_count - 1),
            sems(owner_count - 1),
            sems(owner_count),
            sems(owner_count),
        ],
        compiler_params=pltpu.CompilerParams(
            vmem_limit_bytes=56 << 20, collective_id=0, has_side_effects=True
        ),
        name="search",
    )(raw, proto, *small)
    return box.reshape(capacity, owner_count, 1, trials, widths.shape[0], spec)


def solution(mesh):
    return jax.shard_map(
        functools.partial(shards, mesh.axis_names),
        mesh=mesh,
        in_specs=(P(("group", "dm", "beam"), "tm"), P(), P(), P(), P()),
        out_specs=P("dm", "group", "beam", None, None, "tm"),
        check_vma=False,
    )
```

```python
import functools
import math

import jax
import jax.numpy as jnp
import numpy as np
from jax import lax
from jax.experimental import pallas as pl
from jax.experimental.pallas import tpu as pltpu
from jax.sharding import PartitionSpec as P

SIDE = 128
NBLK = 64
FD = 4
TT = 8
MAXT = 3
WMAX = 8
SPB = 64
FIRST = 4
CHUNK = 16
GROUP = 8
AHEAD = 3
HALF = SIDE // 2
FR = 72
BACK = 128 - TT
MESH = pl.DeviceIdType.MESH
F32 = jnp.float32
BF16 = jnp.bfloat16
FT = BF16


def tables(channels):
    i = np.arange(SIDE)
    ang = (i[:, None] * i[None, :] % SIDE) * (2.0 * math.pi / SIDE)
    c, s = np.cos(ang), np.sin(ang)
    w1 = np.concatenate([c[:HALF], s[:HALF], c[HALF:FR], s[HALF:FR]], 0)
    w2 = np.block([[c, -s], [-s, -c]])
    tw = (i[:, None] * i[None, :] % channels) * (2.0 * math.pi / channels)
    twiddle = np.stack([np.cos(tw[:FR]), np.sin(tw[:FR])]).astype(np.float32)
    return jnp.asarray(w1, BF16), jnp.asarray(w2, BF16), jnp.asarray(twiddle[:, :HALF], BF16), jnp.asarray(twiddle[:, HALF:])


def fine_rows(groups, width):
    g = np.arange(groups)[:, None]
    i = np.arange(width)[None, :]
    fine = g * FD * (width - 1 - i) // (groups * (width - 1))
    hot = np.stack([fine == step for step in range(FD)])
    hot = hot.reshape(FD, groups, width // SIDE, SIDE).transpose(2, 0, 1, 3)
    out = np.zeros((2, 2, FD, groups, FR))
    out[0, ..., : HALF + 1] = hot[..., : HALF + 1]
    out[1, ..., 1:HALF] = hot[..., : HALF : -1]
    return jnp.asarray(out.reshape(-1, FR), BF16)


def iota(shape, dim):
    return lax.broadcasted_iota(jnp.int32, shape, dim)


def search_kernel(
    sizes, raw_ref, proto_ref, w1_any, w2_any, tw_any, last_any, m_any, delays_any, widths_any, owners_any, out_ref,
    xbuf, proto, w1_ref, w2_ref, tw_ref, last_ref, m_ref, delays_ref, widths_ref, owners_ref,
    yone, ytwo, history, p_ref, band_ref, bands, inv, direct, mirror, send, sendb, got, gotb,
    raw_sem, proto_sem, const_sem,
    hist_send, hist_recv, band_send, band_recv, own_send, own_recv, next_send, next_recv,
):
    spectra, spec, groups, slabs, owner_count, axes = sizes
    frame = SIDE * SIDE
    slots = out_ref.shape[0]
    boxes = widths_ref.shape[1]
    trials = out_ref.shape[2] // boxes
    quad = trials * groups
    rows = slots * trials
    tm, dm = lax.axis_index("tm"), lax.axis_index("dm")

    def peer(slab, owner):
        place = {name: lax.axis_index(name) for name in axes}
        place["tm"] = lax.rem(tm + slab, slabs)
        place["dm"] = lax.rem(dm + owner, owner_count)
        return tuple(place[name] for name in axes)

    def remote(src, dst, send_sem, recv_sem, target):
        return pltpu.make_async_remote_copy(
            src_ref=src, dst_ref=dst, send_sem=send_sem, recv_sem=recv_sem,
            device_id=target, device_id_type=MESH,
        )

    def raw_copy(piece):
        start = pl.multiple_of(piece * CHUNK * frame, CHUNK * frame)
        return pltpu.make_async_copy(
            raw_ref.at[:, pl.ds(start, CHUNK * frame)],
            xbuf.at[:, pl.ds(start + 3 * frame, CHUNK * frame)],
            raw_sem.at[piece],
        )

    def history_copy():
        size = history.shape[1]
        last = raw_ref.at[:, pl.ds(spec * frame - size, size)]
        return remote(last, history, hist_send, hist_recv, peer(1, 0))

    barrier = pltpu.get_barrier_semaphore()
    senders = [(off, 0) for off in range(1, slabs)] + [(0, off) for off in range(1, owner_count)]
    if slabs > 1:
        senders += [(slabs - 1, off) for off in range(1, owner_count)]
    for slab, owner in senders:
        pl.semaphore_signal(barrier, inc=1, device_id=peer(slab, owner), device_id_type=MESH)

    constants = [
        pltpu.make_async_copy(src, dst, const_sem.at[n])
        for n, (src, dst) in enumerate(
            [
                (w1_any, w1_ref), (tw_any, tw_ref), (last_any, last_ref), (w2_any, w2_ref), (m_any, m_ref),
                (delays_any, delays_ref), (widths_any, widths_ref), (owners_any, owners_ref),
            ]
        )
    ]
    taps = [
        pltpu.make_async_copy(proto_ref.at[tap : tap + 1], proto.at[tap], proto_sem.at[tap])
        for tap in range(4)
    ]
    raw_copy(0).start()
    for copy in taps:
        copy.start()
    constants[0].start()
    constants[1].start()
    constants[2].start()
    constants[3].start()
    raw_copy(1).start()
    for copy in constants[4:]:
        copy.start()
    for piece in range(2, AHEAD):
        raw_copy(piece).start()
    band_ref[...] = jnp.zeros_like(band_ref)
    xbuf[:, : 3 * frame] = jnp.zeros((1, 3 * frame), BF16)

    tile = 16 * SIDE

    def fir(ybuf, base, tiles, count=CHUNK):
        for r in tiles:
            taps = [proto[tap, :, r * tile : (r + 1) * tile].reshape(16, SIDE).astype(FT) for tap in range(4)]
            seen = []
            for k in range(-3, count):
                start = pl.multiple_of((base + k + 3) * frame + r * tile, tile)
                seen.append(xbuf[:, pl.ds(start, tile)].reshape(16, SIDE).astype(FT))
                if k >= 0:
                    acc = (seen[k] * taps[0] + seen[k + 1] * taps[1]) + (seen[k + 2] * taps[2] + seen[k + 3] * taps[3])
                    ybuf[k // 2, r * 16 : (r + 1) * 16, k % 2 * SIDE : (k % 2 + 1) * SIDE] = acc.astype(BF16)

    def dots(ybuf, base, s, count, keep=None):
        ts = []
        for p in range(s // 2, s // 2 + count):
            a = jnp.dot(w1_ref[...], ybuf[p], preferred_element_type=F32)
            res, ims, tails = [], [], []
            for m in range(2):
                part = a[:, m * SIDE : (m + 1) * SIDE]
                re, im = part[:HALF].astype(BF16), part[HALF : 2 * HALF].astype(BF16)
                res.append(re * tw_ref[0] - im * tw_ref[1])
                ims.append(im * tw_ref[0] + re * tw_ref[1])
                re, im = part[2 * HALF : HALF + FR], part[HALF + FR :]
                tails.append((re * last_ref[0] - im * last_ref[1], im * last_ref[0] + re * last_ref[1]))
            for n, parts in enumerate((res, ims)):
                parts.append(jnp.concatenate([tail[n] for tail in tails], 0).astype(BF16))
            ts.append(jnp.concatenate([jnp.concatenate(res, 0), jnp.concatenate(ims, 0)], 1))
        c = jnp.dot(jnp.concatenate(ts, 0), w2_ref[...], preferred_element_type=F32)
        re, im = c[:, :SIDE], c[:, SIDE:]
        power = re * re + im * im
        parts = []
        for k in range(2 * count):
            top = k // 2 * 2 * FR
            head = top + k % 2 * HALF
            tail = top + 2 * HALF + k % 2 * (FR - HALF)
            parts.append(jnp.concatenate([power[head : head + HALF], power[tail : tail + FR - HALF]], 0))
            p_ref[pl.ds(pl.multiple_of((base + s + k) * FR, FR), FR)] = parts[-1]
        if keep is not None:
            parts[:FIRST] = [jnp.where(keep, part, 0.0) for part in parts[:FIRST]]
        while len(parts) > 1:
            parts = [parts[k] + parts[k + 1] for k in range(0, len(parts), 2)]
        band_ref[...] += parts[0]

    def stage(ybuf, base, ynext, following, keep=None):
        units = CHUNK // (2 * GROUP)
        for u in range(units):
            dots(ybuf, base, 2 * GROUP * u, GROUP, keep if u == 0 else None)
            fir(ynext, following, range(8 * u // units, 8 * (u + 1) // units))

    pl.semaphore_wait(barrier, len(senders))
    if slabs > 1:
        history_copy().start()
    raw_copy(0).wait()
    for copy in taps:
        copy.wait()
    raw_copy(AHEAD).start()
    fir(yone, 0, range(8))
    for copy in constants[:4]:
        copy.wait()

    def chunk(step, carry):
        base = step * (2 * CHUNK)

        def arrive(piece):
            raw_copy(piece).wait()

            @pl.when(piece + AHEAD < pieces)
            def _():
                raw_copy(piece + AHEAD).start()

        arrive(2 * step + 1)
        arrive(2 * step + 2)

        stage(yone, base, ytwo, base + CHUNK, step > 0)
        stage(ytwo, base + CHUNK, yone, base + 2 * CHUNK)
        return carry

    pieces = spec // CHUNK
    steps = pieces // 2
    lax.fori_loop(0, steps - 1, chunk, 0)
    base = spec - 2 * CHUNK
    raw_copy(pieces - 1).wait()
    stage(yone, base, ytwo, base + CHUNK)
    if slabs > 1:
        history_copy().wait()
        xbuf[:, : 3 * frame] = jnp.where(tm > 0, history[...], 0.0)
    fir(yone, 0, range(8), FIRST)
    for s in range(0, CHUNK, 2 * GROUP):
        dots(ytwo, base + CHUNK, s, GROUP)
    dots(yone, 0, 0, FIRST // 2)

    copies = []
    for off in range(1, slabs):
        copy = remote(band_ref, bands.at[off - 1], band_send.at[off - 1], band_recv.at[off - 1], peer(off, 0))
        copy.start()
        copies.append(copy)

    for copy in constants[4:]:
        copy.wait()
    lanes = (MAXT + 1) * quad
    spot = iota((NBLK, SIDE), 0)
    lane = iota((NBLK, SIDE), 1) // 2
    spread = jnp.concatenate([lane == spot, lane == NBLK - 1 - spot], 1).astype(F32).astype(BF16)
    late = jnp.dot(delays_ref[...].astype(F32).astype(BF16), spread, preferred_element_type=F32)
    line = iota((quad, 2 * SIDE), 0) // trials
    masks = [
        jnp.concatenate(
            [
                jnp.where((late == float(v)) & (line == g), 1.0, 0.0)
                for v in range(MAXT + 1)
            ],
            0,
        ).astype(BF16)
        for g in range(groups)
    ]

    def column(ref):
        n = ref.shape[1]
        same = iota((n, n), 0) == iota((n, n), 1)
        return jnp.sum(jnp.where(same, jnp.broadcast_to(ref[...], (n, n)), 0), 1, keepdims=True)

    lane = iota((groups, lanes), 1) % quad
    row = iota((groups, lanes), 0)
    owner = jnp.broadcast_to(column(owners_ref), (groups, lanes))
    mine = jnp.sum(jnp.where(lane // trials == row, owner, 0), 0, keepdims=True)
    rank = jnp.sum(jnp.where((owner == mine) & (row < lane // trials), 1, 0), 0, keepdims=True)
    place = (mine * slots + rank) * trials + lane[:1] % trials
    pack = jnp.where(iota((owner_count * rows, lanes), 0) == place, 1.0, 0.0)
    pack = jnp.concatenate([pack, pack], 1).astype(BF16)

    reach = jnp.broadcast_to(column(widths_ref), (boxes, SIDE))
    root = 1.0 / jnp.sqrt(reach.astype(F32))
    root = jnp.concatenate([root] * rows, 0)
    reach = jnp.concatenate([reach] * rows, 0)
    if WMAX * rows > SIDE:
        reach = jnp.broadcast_to(reach[:, :1], (boxes * rows, WMAX * rows))
    lag = iota((boxes * rows, WMAX * rows), 1)
    series = iota((boxes * rows, WMAX * rows), 0) // boxes
    kernel = jnp.where((lag % rows == series) & (lag // rows < reach), 1.0, 0.0)
    kernel = jnp.concatenate([kernel, kernel], 1).astype(BF16)
    used = (spec + FD - 1) * groups
    direct[used:] = jnp.zeros((direct.shape[0] - used, SIDE), F32)
    mirror[used:] = jnp.zeros((direct.shape[0] - used, SIDE), F32)

    band = band_ref[...]
    for off in range(1, slabs):
        copies[off - 1].wait()
        band = band + bands[off - 1]
    scale = 1.0 / (4 * frame)
    held = iota((FR, SIDE), 0) <= HALF
    inv[...] = jnp.where(held, scale / (band * (scale / spectra) + 1e-06), 0.0)

    even = iota((FD * groups, SIDE), 1) % 2 == 0
    size = FD * groups

    def flat(step, k):
        ratio = p_ref[pl.ds(pl.multiple_of((step * SPB + k) * FR, FR), FR)] * inv[...]
        total = 2.0 * jnp.sum(ratio, 0, keepdims=True) - ratio[:1] - ratio[HALF : HALF + 1]
        mean = jnp.sum(total, 1, keepdims=True) * (1.0 / frame)
        return (ratio - mean).astype(BF16)

    def block(step, carry):
        carry = list(carry)
        for s in range(0, SPB, 2):
            flats = jnp.concatenate([flat(step, s), flat(step, s + 1)], 1)
            r = jnp.dot(m_ref[...], flats, preferred_element_type=F32)
            for m in range(2):
                part = r[:, m * SIDE : (m + 1) * SIDE]
                one = jnp.where(even, part[:size], part[size : 2 * size])
                two = jnp.where(even, part[3 * size :], part[2 * size : 3 * size])
                for n, (ref, new) in enumerate(((direct, one), (mirror, two))):
                    new = [new[d * groups : (d + 1) * groups] for d in range(FD)]
                    held = carry[n * (FD - 1) : (n + 1) * (FD - 1)] + [0.0]
                    at = pl.multiple_of((step * SPB + s + m) * groups, groups)
                    ref[pl.ds(at, groups)] = held[0] + new[0]
                    for d in range(1, FD):
                        carry[n * (FD - 1) + d - 1] = held[d] + new[d]
        return tuple(carry)

    def sweep(first, last):
        zero = jnp.zeros((groups, SIDE), F32)
        return lax.fori_loop(first, last, block, (zero,) * (2 * (FD - 1)))

    def series(first, count):
        each = 0.0
        for g in range(groups):
            picked = pl.ds(first * groups + g, count, stride=groups)
            both = jnp.concatenate([direct[picked, :], mirror[picked, :]], 1).astype(BF16)
            each = each + lax.dot_general(
                both, masks[g], (((1,), (1,)), ((), ())), preferred_element_type=F32
            )
        return each * (1.0 / math.sqrt(SIDE * SIDE // NBLK) / math.sqrt(NBLK))

    def gather(each, skip, count):
        length = skip + count
        padded = each
        if length > each.shape[0]:
            padded = jnp.concatenate([each, jnp.zeros((length - each.shape[0], lanes), F32)], 0)
        value = iota((count, lanes), 1) // quad
        dd = 0.0
        for v in range(MAXT + 1):
            start = skip - v * TT
            if start < 0:
                moved = jnp.concatenate([jnp.zeros((-start, lanes), F32), padded[: count + start]], 0)
            else:
                moved = padded[start : start + count]
            dd = jnp.where(value == v, moved, dd)
        if count < SIDE:
            dd = jnp.concatenate([dd, jnp.zeros((SIDE - count, lanes), F32)], 0)
        high = dd.astype(BF16)
        low = (dd - high.astype(F32)).astype(BF16)
        return lax.dot_general(
            pack, jnp.concatenate([high, low], 1), (((1,), (1,)), ((), ())), preferred_element_type=F32
        )

    blocks = spec // SPB
    middle = blocks // 2
    count = direct.shape[0] // groups
    carry = sweep(middle, blocks)
    for d in range(FD - 1):
        direct[(spec + d) * groups : (spec + d + 1) * groups] = carry[d]
        mirror[(spec + d) * groups : (spec + d + 1) * groups] = carry[FD - 1 + d]
    copies = []
    if slabs > 1:
        reach = (MAXT + 1) * TT
        late = series(spec - reach, count - spec + reach)
        sendb[...] = gather(late, reach - TT, count - spec + reach).reshape(sendb.shape)
        for off in range(owner_count - 1, -1, -1):
            copy = remote(
                sendb.at[lax.rem(dm + off, owner_count)], gotb.at[dm],
                next_send.at[off], next_recv.at[off], peer(1, off),
            )
            copy.start()
            copies.append(copy)
    carry = sweep(0, middle)
    for d in range(FD - 1):
        start = (middle * SPB + d) * groups
        direct[start : start + groups] += carry[d]
        mirror[start : start + groups] += carry[FD - 1 + d]
    send[...] = gather(series(0, spec), 0, spec).reshape(send.shape)
    for off in range(1, owner_count):
        copy = remote(
            send.at[lax.rem(dm + off, owner_count)], got.at[dm],
            own_send.at[off - 1], own_recv.at[off - 1], peer(0, off),
        )
        copy.start()
        copies.append(copy)
    got[dm] = send[dm]
    for copy in copies:
        copy.wait()

    lane = iota((rows, SIDE), 1)
    stacks = []
    for d in range(owner_count):
        own = got[d]
        if slabs > 1:
            past = pltpu.roll(jnp.where(tm > 0, gotb[d], 0.0), SIDE - TT, 1)
            own = own + jnp.where(lane < SIDE - TT, past, 0.0)
        else:
            past = jnp.zeros((rows, SIDE), F32)
        moved = [own]
        for lag in range(1, WMAX):
            moved.append(pltpu.roll(jnp.where(lane < SIDE - lag, own, past), lag, 1))
        stacks.append(jnp.concatenate(moved, 0))
    stack = jnp.concatenate(stacks, 1)
    high = stack.astype(BF16)
    low = (stack - high.astype(F32)).astype(BF16)
    box = jnp.dot(kernel, jnp.concatenate([high, low], 0), preferred_element_type=F32)
    for d in range(owner_count):
        done = (box[:, d * SIDE : (d + 1) * SIDE] * root).astype(BF16)
        for s in range(slots):
            out_ref[s, d] = done[s * trials * boxes : (s + 1) * trials * boxes]


def shards(axes, raw, proto, delays, widths, owners):
    taps, channels = proto.shape
    spec = raw.shape[1] // channels
    groups, trials, _ = delays.shape
    slabs, owner_count = lax.axis_size("tm"), lax.axis_size("dm")
    capacity = 2 * (groups // owner_count)
    w1, w2, tw, last = tables(channels)
    masks = fine_rows(groups, channels // NBLK)
    sizes = (spec * slabs, spec, groups, slabs, owner_count, axes)
    rows = -(-(spec + FD - 1) // 8) * 8
    block = pltpu.VMEM((owner_count, capacity * trials, SIDE), F32)
    sems = lambda n: pltpu.SemaphoreType.DMA((max(n, 1),))
    small = [w1, w2, tw, last, masks, delays.reshape(groups * trials, NBLK), widths[None], owners.T]
    out = (capacity, owner_count, trials * widths.shape[0], spec)
    box = pl.pallas_call(
        functools.partial(search_kernel, sizes),
        in_specs=[pl.BlockSpec(memory_space=pl.ANY)] * (2 + len(small)),
        out_specs=pl.BlockSpec(memory_space=pltpu.VMEM),
        out_shape=pltpu.VMEM(out, BF16),
        scratch_shapes=[
            pltpu.VMEM((1, (spec + 3) * channels), BF16),
            pltpu.VMEM((taps, 1, channels), F32),
            *[pltpu.VMEM(value.shape, value.dtype) for value in small],
            pltpu.VMEM((CHUNK // 2, SIDE, 2 * SIDE), BF16),
            pltpu.VMEM((CHUNK // 2, SIDE, 2 * SIDE), BF16),
            pltpu.VMEM((1, 3 * channels), BF16),
            pltpu.VMEM((spec * FR, SIDE), F32),
            pltpu.VMEM((FR, SIDE), F32),
            pltpu.VMEM((max(slabs - 1, 1), FR, SIDE), F32),
            pltpu.VMEM((FR, SIDE), F32),
            pltpu.VMEM((rows * groups, SIDE), F32),
            pltpu.VMEM((rows * groups, SIDE), F32),
            block,
            block,
            block,
            block,
            sems(spec // CHUNK),
            sems(taps),
            sems(len(small)),
            pltpu.SemaphoreType.DMA,
            pltpu.SemaphoreType.DMA,
            sems(slabs - 1),
            sems(slabs - 1),
            sems(owner_count - 1),
            sems(owner_count - 1),
            sems(owner_count),
            sems(owner_count),
        ],
        compiler_params=pltpu.CompilerParams(
            vmem_limit_bytes=56 << 20, collective_id=0, has_side_effects=True
        ),
        name="search",
    )(raw, proto, *small)
    return box.reshape(capacity, owner_count, 1, trials, widths.shape[0], spec)


def solution(mesh):
    return jax.shard_map(
        functools.partial(shards, mesh.axis_names),
        mesh=mesh,
        in_specs=(P(("group", "dm", "beam"), "tm"), P(), P(), P(), P()),
        out_specs=P("dm", "group", "beam", None, None, "tm"),
        check_vma=False,
    )
```

```python
import functools
import math

import jax
import jax.numpy as jnp
import numpy as np
from jax import lax
from jax.experimental import pallas as pl
from jax.experimental.pallas import tpu as pltpu
from jax.sharding import PartitionSpec as P

SIDE = 128
NBLK = 64
FD = 4
TT = 8
MAXT = 3
WMAX = 8
SPB = 64
FIRST = 4
CHUNK = 16
GROUP = 8
AHEAD = 3
HALF = SIDE // 2
FR = 72
FS = 80
BACK = 128 - TT
MESH = pl.DeviceIdType.MESH
F32 = jnp.float32
BF16 = jnp.bfloat16
FT = BF16


def tables(channels):
    i = np.arange(SIDE)
    ang = (i[:, None] * i[None, :] % SIDE) * (2.0 * math.pi / SIDE)
    c, s = np.cos(ang), np.sin(ang)
    w1 = np.concatenate([c[:HALF], s[:HALF], c[HALF:FR], s[HALF:FR]], 0)
    w2 = np.block([[c, -s], [-s, -c]])
    tw = (i[:, None] * i[None, :] % channels) * (2.0 * math.pi / channels)
    twiddle = np.stack([np.cos(tw[:FR]), np.sin(tw[:FR])]).astype(np.float32)
    return jnp.asarray(w1, BF16), jnp.asarray(w2, BF16), jnp.asarray(twiddle[:, :HALF], BF16), jnp.asarray(twiddle[:, HALF:])


def fine_rows(groups, width):
    g = np.arange(groups)[:, None]
    i = np.arange(width)[None, :]
    fine = g * FD * (width - 1 - i) // (groups * (width - 1))
    hot = np.stack([fine == step for step in range(FD)])
    hot = hot.reshape(FD, groups, width // SIDE, SIDE).transpose(2, 0, 1, 3)
    out = np.zeros((2, 2, FD, groups, FR))
    out[0, ..., : HALF + 1] = hot[..., : HALF + 1]
    out[1, ..., 1:HALF] = hot[..., : HALF : -1]
    return jnp.asarray(out.reshape(-1, FR), BF16)


def iota(shape, dim):
    return lax.broadcasted_iota(jnp.int32, shape, dim)


def search_kernel(
    sizes, raw_ref, proto_ref, w1_any, w2_any, tw_any, last_any, m_any, delays_any, widths_any, owners_any, out_ref,
    xbuf, proto, w1_ref, w2_ref, tw_ref, last_ref, m_ref, delays_ref, widths_ref, owners_ref,
    yone, ytwo, history, p_ref, band_ref, band_out, bands, inv, direct, mirror, send, sendb, got, gotb,
    masks, pack_ref, kernel_ref, root_ref, open_sem, raw_sem, proto_sem, const_sem,
    hist_send, hist_recv, band_send, band_recv, own_send, own_recv, next_send, next_recv,
):
    spectra, spec, groups, slabs, owner_count, axes = sizes
    frame = SIDE * SIDE
    slots = out_ref.shape[0]
    boxes = widths_ref.shape[1]
    trials = out_ref.shape[2] // boxes
    quad = trials * groups
    rows = slots * trials
    tm, dm = lax.axis_index("tm"), lax.axis_index("dm")

    def peer(slab, owner):
        place = {name: lax.axis_index(name) for name in axes}
        place["tm"] = lax.rem(tm + slab, slabs)
        place["dm"] = lax.rem(dm + owner, owner_count)
        return tuple(place[name] for name in axes)

    def remote(src, dst, send_sem, recv_sem, target):
        return pltpu.make_async_remote_copy(
            src_ref=src, dst_ref=dst, send_sem=send_sem, recv_sem=recv_sem,
            device_id=target, device_id_type=MESH,
        )

    def raw_copy(piece):
        start = pl.multiple_of(piece * CHUNK * frame, CHUNK * frame)
        return pltpu.make_async_copy(
            raw_ref.at[:, pl.ds(start, CHUNK * frame)],
            xbuf.at[:, pl.ds(start + 3 * frame, CHUNK * frame)],
            raw_sem.at[piece],
        )

    def opening(half):
        start = half * CHUNK // 2 * frame
        return pltpu.make_async_copy(
            raw_ref.at[:, pl.ds(start, CHUNK // 2 * frame)],
            xbuf.at[:, pl.ds(start + 3 * frame, CHUNK // 2 * frame)],
            open_sem.at[half],
        )

    def history_copy():
        size = history.shape[1]
        last = raw_ref.at[:, pl.ds(spec * frame - size, size)]
        return remote(last, history, hist_send, hist_recv, peer(1, 0))

    taps = [
        pltpu.make_async_copy(proto_ref.at[tap : tap + 1], proto.at[tap], proto_sem.at[tap])
        for tap in range(4)
    ]
    opening(0).start()
    for copy in taps:
        copy.start()
    opening(1).start()
    barrier = pltpu.get_barrier_semaphore()
    senders = [(off, 0) for off in range(1, slabs)] + [(0, off) for off in range(1, owner_count)]
    if slabs > 1:
        senders += [(slabs - 1, off) for off in range(1, owner_count)]
    for slab, owner in senders:
        pl.semaphore_signal(barrier, inc=1, device_id=peer(slab, owner), device_id_type=MESH)

    constants = [
        pltpu.make_async_copy(src, dst, const_sem.at[n])
        for n, (src, dst) in enumerate(
            [
                (w1_any, w1_ref), (tw_any, tw_ref), (last_any, last_ref), (w2_any, w2_ref), (m_any, m_ref),
                (delays_any, delays_ref), (widths_any, widths_ref), (owners_any, owners_ref),
            ]
        )
    ]
    constants[0].start()
    constants[1].start()
    constants[2].start()
    constants[3].start()
    raw_copy(1).start()
    for copy in constants[4:]:
        copy.start()
    for piece in range(2, AHEAD):
        raw_copy(piece).start()
    band_ref[...] = jnp.zeros_like(band_ref)
    xbuf[:, : 3 * frame] = jnp.zeros((1, 3 * frame), BF16)

    tile = 16 * SIDE

    def fir(ybuf, base, tiles, first=0, last=CHUNK):
        for r in tiles:
            taps = [proto[tap, :, r * tile : (r + 1) * tile].reshape(16, SIDE).astype(FT) for tap in range(4)]
            seen = []
            for k in range(first - 3, last):
                start = pl.multiple_of((base + k + 3) * frame + r * tile, tile)
                seen.append(xbuf[:, pl.ds(start, tile)].reshape(16, SIDE).astype(FT))
                if k >= first:
                    acc = (seen[-4] * taps[0] + seen[-3] * taps[1]) + (seen[-2] * taps[2] + seen[-1] * taps[3])
                    ybuf[k // 2, r * 16 : (r + 1) * 16, k % 2 * SIDE : (k % 2 + 1) * SIDE] = acc.astype(BF16)

    def dots(ybuf, base, s, count, keep=None):
        ts = []
        for p in range(s // 2, s // 2 + count):
            a = jnp.dot(w1_ref[...], ybuf[p], preferred_element_type=F32)
            res, ims, tails = [], [], []
            for m in range(2):
                part = a[:, m * SIDE : (m + 1) * SIDE]
                re, im = part[:HALF].astype(BF16), part[HALF : 2 * HALF].astype(BF16)
                res.append(re * tw_ref[0] - im * tw_ref[1])
                ims.append(im * tw_ref[0] + re * tw_ref[1])
                re, im = part[2 * HALF : HALF + FR], part[HALF + FR :]
                tails.append((re * last_ref[0] - im * last_ref[1], im * last_ref[0] + re * last_ref[1]))
            for n, parts in enumerate((res, ims)):
                parts.append(jnp.concatenate([tail[n] for tail in tails], 0).astype(BF16))
            ts.append(jnp.concatenate([jnp.concatenate(res, 0), jnp.concatenate(ims, 0)], 1))
        c = jnp.dot(jnp.concatenate(ts, 0), w2_ref[...], preferred_element_type=F32)
        re, im = c[:, :SIDE], c[:, SIDE:]
        power = re * re + im * im
        parts = []
        for k in range(2 * count):
            top = k // 2 * 2 * FR
            head = top + k % 2 * HALF
            tail = top + 2 * HALF + k % 2 * (FR - HALF)
            parts.append(jnp.concatenate([power[head : head + HALF], power[tail : tail + FR - HALF]], 0))
            p_ref[pl.ds(pl.multiple_of((base + s + k) * FR, FR), FR)] = parts[-1]
        if keep is not None:
            parts[:FIRST] = [jnp.where(keep, part, 0.0) for part in parts[:FIRST]]
        while len(parts) > 1:
            parts = [parts[k] + parts[k + 1] for k in range(0, len(parts), 2)]
        band_ref[...] += parts[0]

    def stage(ybuf, base, ynext, following, keep=None):
        units = CHUNK // (2 * GROUP)
        for u in range(units):
            dots(ybuf, base, 2 * GROUP * u, GROUP, keep if u == 0 else None)
            fir(ynext, following, range(8 * u // units, 8 * (u + 1) // units))

    pl.semaphore_wait(barrier, len(senders))
    if slabs > 1:
        history_copy().start()
    opening(0).wait()
    for copy in taps:
        copy.wait()
    raw_copy(AHEAD).start()
    fir(yone, 0, range(8), 0, CHUNK // 2)
    opening(1).wait()
    fir(yone, 0, range(8), CHUNK // 2, CHUNK)
    for copy in constants[:4]:
        copy.wait()

    def chunk(step, carry):
        base = step * (2 * CHUNK)

        def arrive(piece):
            raw_copy(piece).wait()

            @pl.when(piece + AHEAD < pieces)
            def _():
                raw_copy(piece + AHEAD).start()

        arrive(2 * step + 1)
        arrive(2 * step + 2)

        stage(yone, base, ytwo, base + CHUNK, step > 0)
        stage(ytwo, base + CHUNK, yone, base + 2 * CHUNK)
        return carry

    pieces = spec // CHUNK
    steps = pieces // 2
    lax.fori_loop(0, steps - 1, chunk, 0)
    base = spec - 2 * CHUNK
    raw_copy(pieces - 1).wait()
    stage(yone, base, ytwo, base + CHUNK)
    if slabs > 1:
        history_copy().wait()
        xbuf[:, : 3 * frame] = jnp.where(tm > 0, history[...], 0.0)
    fir(yone, 0, range(8), 0, FIRST)
    for s in range(0, CHUNK, 2 * GROUP):
        dots(ytwo, base + CHUNK, s, GROUP)
    dots(yone, 0, 0, FIRST // 2)

    band_out[...] = jnp.concatenate([band_ref[...], jnp.zeros((FS - FR, SIDE), F32)], 0).astype(BF16)
    copies = []
    for off in range(1, slabs):
        copy = remote(band_out, bands.at[off - 1], band_send.at[off - 1], band_recv.at[off - 1], peer(off, 0))
        copy.start()
        copies.append(copy)

    for copy in constants[4:]:
        copy.wait()
    lanes = (MAXT + 1) * quad
    spot = iota((NBLK, SIDE), 0)
    lane = iota((NBLK, SIDE), 1) // 2
    spread = jnp.concatenate([lane == spot, lane == NBLK - 1 - spot], 1).astype(F32).astype(BF16)
    late = jnp.dot(delays_ref[...].astype(F32).astype(BF16), spread, preferred_element_type=F32)
    line = iota((quad, 2 * SIDE), 0) // trials
    for g in range(groups):
        masks[g] = jnp.concatenate(
            [
                jnp.where((late == float(v)) & (line == g), 1.0, 0.0)
                for v in range(MAXT + 1)
            ],
            0,
        ).astype(BF16)

    def column(ref):
        n = ref.shape[1]
        same = iota((n, n), 0) == iota((n, n), 1)
        return jnp.sum(jnp.where(same, jnp.broadcast_to(ref[...], (n, n)), 0), 1, keepdims=True)

    lane = iota((groups, lanes), 1) % quad
    row = iota((groups, lanes), 0)
    owner = jnp.broadcast_to(column(owners_ref), (groups, lanes))
    mine = jnp.sum(jnp.where(lane // trials == row, owner, 0), 0, keepdims=True)
    rank = jnp.sum(jnp.where((owner == mine) & (row < lane // trials), 1, 0), 0, keepdims=True)
    place = (mine * slots + rank) * trials + lane[:1] % trials
    pack = jnp.where(iota((owner_count * rows, lanes), 0) == place, 1.0, 0.0)
    pack_ref[...] = jnp.concatenate([pack, pack], 1).astype(BF16)

    reach = jnp.broadcast_to(column(widths_ref), (boxes, SIDE))
    root = 1.0 / jnp.sqrt(reach.astype(F32))
    root_ref[...] = jnp.concatenate([root] * rows, 0)
    reach = jnp.concatenate([reach] * rows, 0)
    if WMAX * rows > SIDE:
        reach = jnp.broadcast_to(reach[:, :1], (boxes * rows, WMAX * rows))
    lag = iota((boxes * rows, WMAX * rows), 1)
    series = iota((boxes * rows, WMAX * rows), 0) // boxes
    kernel = jnp.where((lag % rows == series) & (lag // rows < reach), 1.0, 0.0)
    kernel_ref[...] = kernel.astype(BF16)
    used = (spec + FD - 1) * groups
    direct[used:] = jnp.zeros((direct.shape[0] - used, SIDE), F32)
    mirror[used:] = jnp.zeros((direct.shape[0] - used, SIDE), F32)

    band = band_ref[...]
    for off in range(1, slabs):
        copies[off - 1].wait()
        band = band + bands[off - 1].astype(F32)[:FR]
    scale = 1.0 / (4 * frame)
    held = iota((FR, SIDE), 0) <= HALF
    inv[...] = jnp.where(held, scale / (band * (scale / spectra) + 1e-06), 0.0)

    even = iota((FD * groups, SIDE), 1) % 2 == 0
    size = FD * groups

    def flat(step, k):
        ratio = p_ref[pl.ds(pl.multiple_of((step * SPB + k) * FR, FR), FR)] * inv[...]
        total = 2.0 * jnp.sum(ratio, 0, keepdims=True) - ratio[:1] - ratio[HALF : HALF + 1]
        mean = jnp.sum(total, 1, keepdims=True) * (1.0 / frame)
        return (ratio - mean).astype(BF16)

    def block(step, carry):
        carry = list(carry)
        for s in range(0, SPB, 2):
            flats = jnp.concatenate([flat(step, s), flat(step, s + 1)], 1)
            r = jnp.dot(m_ref[...], flats, preferred_element_type=F32)
            for m in range(2):
                part = r[:, m * SIDE : (m + 1) * SIDE]
                one = jnp.where(even, part[:size], part[size : 2 * size])
                two = jnp.where(even, part[3 * size :], part[2 * size : 3 * size])
                for n, (ref, new) in enumerate(((direct, one), (mirror, two))):
                    new = [new[d * groups : (d + 1) * groups] for d in range(FD)]
                    held = carry[n * (FD - 1) : (n + 1) * (FD - 1)] + [0.0]
                    at = pl.multiple_of((step * SPB + s + m) * groups, groups)
                    ref[pl.ds(at, groups)] = held[0] + new[0]
                    for d in range(1, FD):
                        carry[n * (FD - 1) + d - 1] = held[d] + new[d]
        return tuple(carry)

    def sweep(first, last):
        zero = jnp.zeros((groups, SIDE), F32)
        return lax.fori_loop(first, last, block, (zero,) * (2 * (FD - 1)))

    def series(first, count):
        each = 0.0
        for g in range(groups):
            picked = pl.ds(first * groups + g, count, stride=groups)
            both = jnp.concatenate([direct[picked, :], mirror[picked, :]], 1).astype(BF16)
            each = each + lax.dot_general(
                both, masks[g], (((1,), (1,)), ((), ())), preferred_element_type=F32
            )
        return each * (1.0 / math.sqrt(SIDE * SIDE // NBLK) / math.sqrt(NBLK))

    def gather(each, skip, count):
        length = skip + count
        padded = each
        if length > each.shape[0]:
            padded = jnp.concatenate([each, jnp.zeros((length - each.shape[0], lanes), F32)], 0)
        value = iota((count, lanes), 1) // quad
        dd = 0.0
        for v in range(MAXT + 1):
            start = skip - v * TT
            if start < 0:
                moved = jnp.concatenate([jnp.zeros((-start, lanes), F32), padded[: count + start]], 0)
            else:
                moved = padded[start : start + count]
            dd = jnp.where(value == v, moved, dd)
        if count < SIDE:
            dd = jnp.concatenate([dd, jnp.zeros((SIDE - count, lanes), F32)], 0)
        high = dd.astype(BF16)
        low = (dd - high.astype(F32)).astype(BF16)
        return lax.dot_general(
            pack_ref[...], jnp.concatenate([high, low], 1), (((1,), (1,)), ((), ())), preferred_element_type=F32
        )

    blocks = spec // SPB
    middle = blocks // 2
    count = direct.shape[0] // groups
    carry = sweep(middle, blocks)
    for d in range(FD - 1):
        direct[(spec + d) * groups : (spec + d + 1) * groups] = carry[d]
        mirror[(spec + d) * groups : (spec + d + 1) * groups] = carry[FD - 1 + d]
    copies = []
    half = middle * SPB
    upper = series(half, count - half)
    if slabs > 1:
        reach = (MAXT + 1) * TT
        late = upper[spec - reach - half :]
        sendb[...] = gather(late, reach - TT, count - spec + reach).reshape(sendb.shape).astype(BF16)
        for off in range(owner_count - 1, -1, -1):
            copy = remote(
                sendb.at[lax.rem(dm + off, owner_count)], gotb.at[dm],
                next_send.at[off], next_recv.at[off], peer(1, off),
            )
            copy.start()
            copies.append(copy)
    carry = sweep(0, middle)
    for d in range(FD - 1):
        start = (middle * SPB + d) * groups
        direct[start : start + groups] += carry[d]
        mirror[start : start + groups] += carry[FD - 1 + d]
    lower = series(0, half + 16)
    each = jnp.concatenate([lower, upper[16 : spec - half]], 0)
    send[...] = gather(each, 0, spec).reshape(send.shape).astype(BF16)
    for off in range(1, owner_count):
        copy = remote(
            send.at[lax.rem(dm + off, owner_count)], got.at[dm],
            own_send.at[off - 1], own_recv.at[off - 1], peer(0, off),
        )
        copy.start()
        copies.append(copy)
    got[dm] = send[dm]
    for copy in copies:
        copy.wait()

    lane = iota((rows, SIDE), 1)
    stacks = []
    for d in range(owner_count):
        own = got[d].astype(F32)
        if slabs > 1:
            past = pltpu.roll(jnp.where(tm > 0, gotb[d].astype(F32), 0.0), SIDE - TT, 1)
            own = own + jnp.where(lane < SIDE - TT, past, 0.0)
        else:
            past = jnp.zeros((rows, SIDE), F32)
        moved = [own]
        for lag in range(1, WMAX):
            moved.append(pltpu.roll(jnp.where(lane < SIDE - lag, own, past), lag, 1))
        stacks.append(jnp.concatenate(moved, 0))
    stack = jnp.concatenate(stacks, 1).astype(BF16)
    box = jnp.dot(kernel_ref[...], stack, preferred_element_type=F32)
    for d in range(owner_count):
        done = (box[:, d * SIDE : (d + 1) * SIDE] * root_ref[...]).astype(BF16)
        for s in range(slots):
            out_ref[s, d] = done[s * trials * boxes : (s + 1) * trials * boxes]


def shards(axes, raw, proto, delays, widths, owners):
    taps, channels = proto.shape
    spec = raw.shape[1] // channels
    groups, trials, _ = delays.shape
    slabs, owner_count = lax.axis_size("tm"), lax.axis_size("dm")
    capacity = 2 * (groups // owner_count)
    w1, w2, tw, last = tables(channels)
    masks = fine_rows(groups, channels // NBLK)
    sizes = (spec * slabs, spec, groups, slabs, owner_count, axes)
    rows = -(-(spec + FD - 1) // 8) * 8
    lanes = (MAXT + 1) * groups * trials
    boxes = widths.shape[0]
    block = pltpu.VMEM((owner_count, capacity * trials, SIDE), BF16)
    sems = lambda n: pltpu.SemaphoreType.DMA((max(n, 1),))
    small = [w1, w2, tw, last, masks, delays.reshape(groups * trials, NBLK), widths[None], owners.T]
    out = (capacity, owner_count, trials * widths.shape[0], spec)
    box = pl.pallas_call(
        functools.partial(search_kernel, sizes),
        in_specs=[pl.BlockSpec(memory_space=pl.ANY)] * (2 + len(small)),
        out_specs=pl.BlockSpec(memory_space=pltpu.VMEM),
        out_shape=pltpu.VMEM(out, BF16),
        scratch_shapes=[
            pltpu.VMEM((1, (spec + 3) * channels), BF16),
            pltpu.VMEM((taps, 1, channels), F32),
            *[pltpu.VMEM(value.shape, value.dtype) for value in small],
            pltpu.VMEM((CHUNK // 2, SIDE, 2 * SIDE), BF16),
            pltpu.VMEM((CHUNK // 2, SIDE, 2 * SIDE), BF16),
            pltpu.VMEM((1, 3 * channels), BF16),
            pltpu.VMEM((spec * FR, SIDE), F32),
            pltpu.VMEM((FR, SIDE), F32),
            pltpu.VMEM((FS, SIDE), BF16),
            pltpu.VMEM((max(slabs - 1, 1), FS, SIDE), BF16),
            pltpu.VMEM((FR, SIDE), F32),
            pltpu.VMEM((rows * groups, SIDE), F32),
            pltpu.VMEM((rows * groups, SIDE), F32),
            block,
            block,
            block,
            block,
            pltpu.VMEM((groups, lanes, 2 * SIDE), BF16),
            pltpu.VMEM((owner_count * capacity * trials, 2 * lanes), BF16),
            pltpu.VMEM((boxes * capacity * trials, WMAX * capacity * trials), BF16),
            pltpu.VMEM((boxes * capacity * trials, SIDE), F32),
            sems(2),
            sems(spec // CHUNK),
            sems(taps),
            sems(len(small)),
            pltpu.SemaphoreType.DMA,
            pltpu.SemaphoreType.DMA,
            sems(slabs - 1),
            sems(slabs - 1),
            sems(owner_count - 1),
            sems(owner_count - 1),
            sems(owner_count),
            sems(owner_count),
        ],
        compiler_params=pltpu.CompilerParams(
            vmem_limit_bytes=56 << 20, collective_id=0, has_side_effects=True
        ),
        name="search",
    )(raw, proto, *small)
    return box.reshape(capacity, owner_count, 1, trials, widths.shape[0], spec)


def solution(mesh):
    return jax.shard_map(
        functools.partial(shards, mesh.axis_names),
        mesh=mesh,
        in_specs=(P(("group", "dm", "beam"), "tm"), P(), P(), P(), P()),
        out_specs=P("dm", "group", "beam", None, None, "tm"),
        check_vma=False,
    )
```

```python
import functools
import math

import jax
import jax.numpy as jnp
import numpy as np
from jax import lax
from jax.experimental import pallas as pl
from jax.experimental.pallas import tpu as pltpu
from jax.sharding import PartitionSpec as P

SIDE = 128
NBLK = 64
FD = 4
TT = 8
MAXT = 3
WMAX = 8
SPB = 64
FIRST = 4
CHUNK = 16
GROUP = 8
AHEAD = 3
HALF = SIDE // 2
FR = 72
FS = 80
BACK = 128 - TT
MESH = pl.DeviceIdType.MESH
F32 = jnp.float32
BF16 = jnp.bfloat16
FT = BF16


def tables(channels):
    i = np.arange(SIDE)
    ang = (i[:, None] * i[None, :] % SIDE) * (2.0 * math.pi / SIDE)
    c, s = np.cos(ang), np.sin(ang)
    w1 = np.concatenate([c[:HALF], s[:HALF], c[HALF:FR], s[HALF:FR]], 0)
    w2 = np.block([[c, -s], [-s, -c]])
    tw = (i[:, None] * i[None, :] % channels) * (2.0 * math.pi / channels)
    twiddle = np.stack([np.cos(tw[:FR]), np.sin(tw[:FR])]).astype(np.float32)
    return jnp.asarray(w1, BF16), jnp.asarray(w2, BF16), jnp.asarray(twiddle[:, :HALF], BF16), jnp.asarray(twiddle[:, HALF:])


def fine_rows(groups, width):
    g = np.arange(groups)[:, None]
    i = np.arange(width)[None, :]
    fine = g * FD * (width - 1 - i) // (groups * (width - 1))
    hot = np.stack([fine == step for step in range(FD)])
    hot = hot.reshape(FD, groups, width // SIDE, SIDE).transpose(2, 0, 1, 3)
    out = np.zeros((2, 2, FD, groups, FR))
    out[0, ..., : HALF + 1] = hot[..., : HALF + 1]
    out[1, ..., 1:HALF] = hot[..., : HALF : -1]
    return jnp.asarray(out.reshape(-1, FR), BF16)


def iota(shape, dim):
    return lax.broadcasted_iota(jnp.int32, shape, dim)


def search_kernel(
    sizes, raw_ref, proto_ref, w1_any, w2_any, tw_any, last_any, m_any, delays_any, widths_any, owners_any, out_ref,
    xbuf, proto, w1_ref, w2_ref, tw_ref, last_ref, m_ref, delays_ref, widths_ref, owners_ref,
    yone, ytwo, hist_raw, hist_out, history, p_ref, band_ref, band_out, bands, inv, direct, mirror, send, sendb, got, gotb,
    masks, pack_ref, kernel_ref, root_ref, open_sem, raw_sem, proto_sem, const_sem,
    hist_send, hist_recv, band_send, band_recv, own_send, own_recv, next_send, next_recv,
):
    spectra, spec, groups, slabs, owner_count, axes = sizes
    frame = SIDE * SIDE
    slots = out_ref.shape[0]
    boxes = widths_ref.shape[1]
    trials = out_ref.shape[2] // boxes
    quad = trials * groups
    rows = slots * trials
    tm, dm = lax.axis_index("tm"), lax.axis_index("dm")

    def peer(slab, owner):
        place = {name: lax.axis_index(name) for name in axes}
        place["tm"] = lax.rem(tm + slab, slabs)
        place["dm"] = lax.rem(dm + owner, owner_count)
        return tuple(place[name] for name in axes)

    def remote(src, dst, send_sem, recv_sem, target):
        return pltpu.make_async_remote_copy(
            src_ref=src, dst_ref=dst, send_sem=send_sem, recv_sem=recv_sem,
            device_id=target, device_id_type=MESH,
        )

    def raw_copy(piece):
        start = pl.multiple_of(piece * CHUNK * frame, CHUNK * frame)
        return pltpu.make_async_copy(
            raw_ref.at[:, pl.ds(start, CHUNK * frame)],
            xbuf.at[:, pl.ds(start + 3 * frame, CHUNK * frame)],
            raw_sem.at[piece],
        )

    def opening(half):
        start = half * CHUNK // 2 * frame
        return pltpu.make_async_copy(
            raw_ref.at[:, pl.ds(start, CHUNK // 2 * frame)],
            xbuf.at[:, pl.ds(start + 3 * frame, CHUNK // 2 * frame)],
            open_sem.at[half],
        )

    def history_copy():
        return remote(hist_out, history, hist_send, hist_recv, peer(1, 0))

    ending = pltpu.make_async_copy(
        raw_ref.at[:, pl.ds((spec - 3) * frame, 3 * frame)], hist_raw, open_sem.at[2]
    )
    if slabs > 1:
        ending.start()
    taps = [
        pltpu.make_async_copy(proto_ref.at[tap : tap + 1], proto.at[tap], proto_sem.at[tap])
        for tap in range(4)
    ]
    opening(0).start()
    for copy in taps:
        copy.start()
    opening(1).start()
    barrier = pltpu.get_barrier_semaphore()
    senders = [(off, 0) for off in range(1, slabs)] + [(0, off) for off in range(1, owner_count)]
    if slabs > 1:
        senders += [(slabs - 1, off) for off in range(1, owner_count)]
    for slab, owner in senders:
        pl.semaphore_signal(barrier, inc=1, device_id=peer(slab, owner), device_id_type=MESH)

    constants = [
        pltpu.make_async_copy(src, dst, const_sem.at[n])
        for n, (src, dst) in enumerate(
            [
                (w1_any, w1_ref), (tw_any, tw_ref), (last_any, last_ref), (w2_any, w2_ref), (m_any, m_ref),
                (delays_any, delays_ref), (widths_any, widths_ref), (owners_any, owners_ref),
            ]
        )
    ]
    constants[0].start()
    constants[1].start()
    constants[2].start()
    constants[3].start()
    raw_copy(1).start()
    for copy in constants[4:]:
        copy.start()
    for piece in range(2, AHEAD):
        raw_copy(piece).start()
    band_ref[...] = jnp.zeros_like(band_ref)
    xbuf[:, : 3 * frame] = jnp.zeros((1, 3 * frame), BF16)

    tile = 16 * SIDE

    def fir(ybuf, base, tiles, first=0, last=CHUNK, past=False):
        for r in tiles:
            taps = [proto[tap, :, r * tile : (r + 1) * tile].reshape(16, SIDE).astype(FT) for tap in range(4)]
            seen = []
            for k in range(first - 3, last):
                if past and k < 0:
                    row = (k + 3) * SIDE + r * 16
                    seen.append(jnp.where(tm > 0, history[row : row + 16].astype(F32), 0.0).astype(FT))
                    continue
                start = pl.multiple_of((base + k + 3) * frame + r * tile, tile)
                seen.append(xbuf[:, pl.ds(start, tile)].reshape(16, SIDE).astype(FT))
                if k >= first:
                    acc = (seen[-4] * taps[0] + seen[-3] * taps[1]) + (seen[-2] * taps[2] + seen[-1] * taps[3])
                    ybuf[k // 2, r * 16 : (r + 1) * 16, k % 2 * SIDE : (k % 2 + 1) * SIDE] = acc.astype(BF16)

    def dots(ybuf, base, s, count, keep=None):
        ts = []
        for p in range(s // 2, s // 2 + count):
            a = jnp.dot(w1_ref[...], ybuf[p], preferred_element_type=F32)
            res, ims, tails = [], [], []
            for m in range(2):
                part = a[:, m * SIDE : (m + 1) * SIDE]
                re, im = part[:HALF].astype(BF16), part[HALF : 2 * HALF].astype(BF16)
                res.append(re * tw_ref[0] - im * tw_ref[1])
                ims.append(im * tw_ref[0] + re * tw_ref[1])
                re, im = part[2 * HALF : HALF + FR], part[HALF + FR :]
                tails.append((re * last_ref[0] - im * last_ref[1], im * last_ref[0] + re * last_ref[1]))
            for n, parts in enumerate((res, ims)):
                parts.append(jnp.concatenate([tail[n] for tail in tails], 0).astype(BF16))
            ts.append(jnp.concatenate([jnp.concatenate(res, 0), jnp.concatenate(ims, 0)], 1))
        c = jnp.dot(jnp.concatenate(ts, 0), w2_ref[...], preferred_element_type=F32)
        re, im = c[:, :SIDE], c[:, SIDE:]
        power = re * re + im * im
        parts = []
        for k in range(2 * count):
            top = k // 2 * 2 * FR
            head = top + k % 2 * HALF
            tail = top + 2 * HALF + k % 2 * (FR - HALF)
            parts.append(jnp.concatenate([power[head : head + HALF], power[tail : tail + FR - HALF]], 0))
            p_ref[pl.ds(pl.multiple_of((base + s + k) * FR, FR), FR)] = parts[-1]
        if keep is not None:
            parts[:FIRST] = [jnp.where(keep, part, 0.0) for part in parts[:FIRST]]
        while len(parts) > 1:
            parts = [parts[k] + parts[k + 1] for k in range(0, len(parts), 2)]
        band_ref[...] += parts[0]

    def stage(ybuf, base, ynext, following, keep=None):
        units = CHUNK // (2 * GROUP)
        for u in range(units):
            dots(ybuf, base, 2 * GROUP * u, GROUP, keep if u == 0 else None)
            fir(ynext, following, range(8 * u // units, 8 * (u + 1) // units))

    if slabs > 1:
        ending.wait()
        hist_out[...] = hist_raw[...].reshape(3 * SIDE, SIDE)
    pl.semaphore_wait(barrier, len(senders))
    if slabs > 1:
        history_copy().start()
    opening(0).wait()
    for copy in taps:
        copy.wait()
    raw_copy(AHEAD).start()
    fir(yone, 0, range(8), 0, CHUNK // 2)
    opening(1).wait()
    fir(yone, 0, range(8), CHUNK // 2, CHUNK)
    for copy in constants[:4]:
        copy.wait()

    def chunk(step, carry):
        base = step * (2 * CHUNK)

        def arrive(piece):
            raw_copy(piece).wait()

            @pl.when(piece + AHEAD < pieces)
            def _():
                raw_copy(piece + AHEAD).start()

        arrive(2 * step + 1)
        arrive(2 * step + 2)

        stage(yone, base, ytwo, base + CHUNK, step > 0)
        stage(ytwo, base + CHUNK, yone, base + 2 * CHUNK)
        return carry

    pieces = spec // CHUNK
    steps = pieces // 2
    lax.fori_loop(0, steps - 1, chunk, 0)
    base = spec - 2 * CHUNK
    raw_copy(pieces - 1).wait()
    stage(yone, base, ytwo, base + CHUNK)
    if slabs > 1:
        history_copy().wait()
    fir(yone, 0, range(8), 0, FIRST, slabs > 1)
    for s in range(0, CHUNK, 2 * GROUP):
        dots(ytwo, base + CHUNK, s, GROUP)
    dots(yone, 0, 0, FIRST // 2)

    band_out[...] = jnp.concatenate([band_ref[...], jnp.zeros((FS - FR, SIDE), F32)], 0).astype(BF16)
    copies = []
    for off in range(1, slabs):
        copy = remote(band_out, bands.at[off - 1], band_send.at[off - 1], band_recv.at[off - 1], peer(off, 0))
        copy.start()
        copies.append(copy)

    for copy in constants[4:]:
        copy.wait()
    lanes = (MAXT + 1) * quad
    spot = iota((NBLK, SIDE), 0)
    lane = iota((NBLK, SIDE), 1) // 2
    spread = jnp.concatenate([lane == spot, lane == NBLK - 1 - spot], 1).astype(F32).astype(BF16)
    late = jnp.dot(delays_ref[...].astype(F32).astype(BF16), spread, preferred_element_type=F32)
    line = iota((quad, 2 * SIDE), 0) // trials
    for g in range(groups):
        masks[g] = jnp.concatenate(
            [
                jnp.where((late == float(v)) & (line == g), 1.0, 0.0)
                for v in range(MAXT + 1)
            ],
            0,
        ).astype(BF16)

    def column(ref):
        n = ref.shape[1]
        same = iota((n, n), 0) == iota((n, n), 1)
        return jnp.sum(jnp.where(same, jnp.broadcast_to(ref[...], (n, n)), 0), 1, keepdims=True)

    lane = iota((groups, lanes), 1) % quad
    row = iota((groups, lanes), 0)
    owner = jnp.broadcast_to(column(owners_ref), (groups, lanes))
    mine = jnp.sum(jnp.where(lane // trials == row, owner, 0), 0, keepdims=True)
    rank = jnp.sum(jnp.where((owner == mine) & (row < lane // trials), 1, 0), 0, keepdims=True)
    place = (mine * slots + rank) * trials + lane[:1] % trials
    pack = jnp.where(iota((owner_count * rows, lanes), 0) == place, 1.0, 0.0)
    pack_ref[...] = jnp.concatenate([pack, pack], 1).astype(BF16)

    reach = jnp.broadcast_to(column(widths_ref), (boxes, SIDE))
    root = 1.0 / jnp.sqrt(reach.astype(F32))
    root_ref[...] = jnp.concatenate([root] * rows, 0)
    reach = jnp.concatenate([reach] * rows, 0)
    if WMAX * rows > SIDE:
        reach = jnp.broadcast_to(reach[:, :1], (boxes * rows, WMAX * rows))
    lag = iota((boxes * rows, WMAX * rows), 1)
    series = iota((boxes * rows, WMAX * rows), 0) // boxes
    kernel = jnp.where((lag % rows == series) & (lag // rows < reach), 1.0, 0.0)
    kernel_ref[...] = kernel.astype(BF16)
    used = (spec + FD - 1) * groups
    direct[used:] = jnp.zeros((direct.shape[0] - used, SIDE), F32)
    mirror[used:] = jnp.zeros((direct.shape[0] - used, SIDE), F32)

    band = band_ref[...]
    for off in range(1, slabs):
        copies[off - 1].wait()
        band = band + bands[off - 1].astype(F32)[:FR]
    scale = 1.0 / (4 * frame)
    held = iota((FR, SIDE), 0) <= HALF
    inv[...] = jnp.where(held, scale / (band * (scale / spectra) + 1e-06), 0.0)

    even = iota((FD * groups, SIDE), 1) % 2 == 0
    size = FD * groups

    def flat(step, k):
        ratio = p_ref[pl.ds(pl.multiple_of((step * SPB + k) * FR, FR), FR)] * inv[...]
        total = 2.0 * jnp.sum(ratio, 0, keepdims=True) - ratio[:1] - ratio[HALF : HALF + 1]
        mean = jnp.sum(total, 1, keepdims=True) * (1.0 / frame)
        return (ratio - mean).astype(BF16)

    def block(step, carry):
        carry = list(carry)
        for s in range(0, SPB, 2):
            flats = jnp.concatenate([flat(step, s), flat(step, s + 1)], 1)
            r = jnp.dot(m_ref[...], flats, preferred_element_type=F32)
            for m in range(2):
                part = r[:, m * SIDE : (m + 1) * SIDE]
                one = jnp.where(even, part[:size], part[size : 2 * size])
                two = jnp.where(even, part[3 * size :], part[2 * size : 3 * size])
                for n, (ref, new) in enumerate(((direct, one), (mirror, two))):
                    new = [new[d * groups : (d + 1) * groups] for d in range(FD)]
                    held = carry[n * (FD - 1) : (n + 1) * (FD - 1)] + [0.0]
                    at = pl.multiple_of((step * SPB + s + m) * groups, groups)
                    ref[pl.ds(at, groups)] = held[0] + new[0]
                    for d in range(1, FD):
                        carry[n * (FD - 1) + d - 1] = held[d] + new[d]
        return tuple(carry)

    def sweep(first, last):
        zero = jnp.zeros((groups, SIDE), F32)
        return lax.fori_loop(first, last, block, (zero,) * (2 * (FD - 1)))

    def series(first, count):
        each = 0.0
        for g in range(groups):
            picked = pl.ds(first * groups + g, count, stride=groups)
            both = jnp.concatenate([direct[picked, :], mirror[picked, :]], 1).astype(BF16)
            each = each + lax.dot_general(
                both, masks[g], (((1,), (1,)), ((), ())), preferred_element_type=F32
            )
        return each * (1.0 / math.sqrt(SIDE * SIDE // NBLK) / math.sqrt(NBLK))

    def gather(each, skip, count):
        length = skip + count
        padded = each
        if length > each.shape[0]:
            padded = jnp.concatenate([each, jnp.zeros((length - each.shape[0], lanes), F32)], 0)
        value = iota((count, lanes), 1) // quad
        dd = 0.0
        for v in range(MAXT + 1):
            start = skip - v * TT
            if start < 0:
                moved = jnp.concatenate([jnp.zeros((-start, lanes), F32), padded[: count + start]], 0)
            else:
                moved = padded[start : start + count]
            dd = jnp.where(value == v, moved, dd)
        if count < SIDE:
            dd = jnp.concatenate([dd, jnp.zeros((SIDE - count, lanes), F32)], 0)
        high = dd.astype(BF16)
        low = (dd - high.astype(F32)).astype(BF16)
        return lax.dot_general(
            pack_ref[...], jnp.concatenate([high, low], 1), (((1,), (1,)), ((), ())), preferred_element_type=F32
        )

    blocks = spec // SPB
    middle = blocks // 2
    count = direct.shape[0] // groups
    carry = sweep(middle, blocks)
    for d in range(FD - 1):
        direct[(spec + d) * groups : (spec + d + 1) * groups] = carry[d]
        mirror[(spec + d) * groups : (spec + d + 1) * groups] = carry[FD - 1 + d]
    copies = []
    half = middle * SPB
    upper = series(half, count - half)
    if slabs > 1:
        reach = (MAXT + 1) * TT
        late = upper[spec - reach - half :]
        sendb[...] = gather(late, reach - TT, count - spec + reach).reshape(sendb.shape).astype(BF16)
        for off in range(owner_count - 1, -1, -1):
            copy = remote(
                sendb.at[lax.rem(dm + off, owner_count)], gotb.at[dm],
                next_send.at[off], next_recv.at[off], peer(1, off),
            )
            copy.start()
            copies.append(copy)
    carry = sweep(0, middle)
    for d in range(FD - 1):
        start = (middle * SPB + d) * groups
        direct[start : start + groups] += carry[d]
        mirror[start : start + groups] += carry[FD - 1 + d]
    lower = series(0, half + 16)
    each = jnp.concatenate([lower, upper[16 : spec - half]], 0)
    send[...] = gather(each, 0, spec).reshape(send.shape).astype(BF16)
    for off in range(1, owner_count):
        copy = remote(
            send.at[lax.rem(dm + off, owner_count)], got.at[dm],
            own_send.at[off - 1], own_recv.at[off - 1], peer(0, off),
        )
        copy.start()
        copies.append(copy)
    got[dm] = send[dm]
    for copy in copies:
        copy.wait()

    lane = iota((rows, SIDE), 1)
    stacks = []
    for d in range(owner_count):
        own = got[d].astype(F32)
        if slabs > 1:
            past = pltpu.roll(jnp.where(tm > 0, gotb[d].astype(F32), 0.0), SIDE - TT, 1)
            own = own + jnp.where(lane < SIDE - TT, past, 0.0)
        else:
            past = jnp.zeros((rows, SIDE), F32)
        moved = [own]
        for lag in range(1, WMAX):
            moved.append(pltpu.roll(jnp.where(lane < SIDE - lag, own, past), lag, 1))
        stacks.append(jnp.concatenate(moved, 0))
    stack = jnp.concatenate(stacks, 1).astype(BF16)
    box = jnp.dot(kernel_ref[...], stack, preferred_element_type=F32)
    for d in range(owner_count):
        done = (box[:, d * SIDE : (d + 1) * SIDE] * root_ref[...]).astype(BF16)
        for s in range(slots):
            out_ref[s, d] = done[s * trials * boxes : (s + 1) * trials * boxes]


def shards(axes, raw, proto, delays, widths, owners):
    taps, channels = proto.shape
    spec = raw.shape[1] // channels
    groups, trials, _ = delays.shape
    slabs, owner_count = lax.axis_size("tm"), lax.axis_size("dm")
    capacity = 2 * (groups // owner_count)
    w1, w2, tw, last = tables(channels)
    masks = fine_rows(groups, channels // NBLK)
    sizes = (spec * slabs, spec, groups, slabs, owner_count, axes)
    rows = -(-(spec + FD - 1) // 8) * 8
    lanes = (MAXT + 1) * groups * trials
    boxes = widths.shape[0]
    block = pltpu.VMEM((owner_count, capacity * trials, SIDE), BF16)
    sems = lambda n: pltpu.SemaphoreType.DMA((max(n, 1),))
    small = [w1, w2, tw, last, masks, delays.reshape(groups * trials, NBLK), widths[None], owners.T]
    out = (capacity, owner_count, trials * widths.shape[0], spec)
    box = pl.pallas_call(
        functools.partial(search_kernel, sizes),
        in_specs=[pl.BlockSpec(memory_space=pl.ANY)] * (2 + len(small)),
        out_specs=pl.BlockSpec(memory_space=pltpu.VMEM),
        out_shape=pltpu.VMEM(out, BF16),
        scratch_shapes=[
            pltpu.VMEM((1, (spec + 3) * channels), BF16),
            pltpu.VMEM((taps, 1, channels), F32),
            *[pltpu.VMEM(value.shape, value.dtype) for value in small],
            pltpu.VMEM((CHUNK // 2, SIDE, 2 * SIDE), BF16),
            pltpu.VMEM((CHUNK // 2, SIDE, 2 * SIDE), BF16),
            pltpu.VMEM((1, 3 * channels), BF16),
            pltpu.VMEM((3 * SIDE, SIDE), BF16),
            pltpu.VMEM((3 * SIDE, SIDE), BF16),
            pltpu.VMEM((spec * FR, SIDE), F32),
            pltpu.VMEM((FR, SIDE), F32),
            pltpu.VMEM((FS, SIDE), BF16),
            pltpu.VMEM((max(slabs - 1, 1), FS, SIDE), BF16),
            pltpu.VMEM((FR, SIDE), F32),
            pltpu.VMEM((rows * groups, SIDE), F32),
            pltpu.VMEM((rows * groups, SIDE), F32),
            block,
            block,
            block,
            block,
            pltpu.VMEM((groups, lanes, 2 * SIDE), BF16),
            pltpu.VMEM((owner_count * capacity * trials, 2 * lanes), BF16),
            pltpu.VMEM((boxes * capacity * trials, WMAX * capacity * trials), BF16),
            pltpu.VMEM((boxes * capacity * trials, SIDE), F32),
            sems(3),
            sems(spec // CHUNK),
            sems(taps),
            sems(len(small)),
            pltpu.SemaphoreType.DMA,
            pltpu.SemaphoreType.DMA,
            sems(slabs - 1),
            sems(slabs - 1),
            sems(owner_count - 1),
            sems(owner_count - 1),
            sems(owner_count),
            sems(owner_count),
        ],
        compiler_params=pltpu.CompilerParams(
            vmem_limit_bytes=56 << 20, collective_id=0, has_side_effects=True
        ),
        name="search",
    )(raw, proto, *small)
    return box.reshape(capacity, owner_count, 1, trials, widths.shape[0], spec)


def solution(mesh):
    return jax.shard_map(
        functools.partial(shards, mesh.axis_names),
        mesh=mesh,
        in_specs=(P(("group", "dm", "beam"), "tm"), P(), P(), P(), P()),
        out_specs=P("dm", "group", "beam", None, None, "tm"),
        check_vma=False,
    )
```

```python
import functools
import math

import jax
import jax.numpy as jnp
import numpy as np
from jax import lax
from jax.experimental import pallas as pl
from jax.experimental.pallas import tpu as pltpu
from jax.sharding import PartitionSpec as P

SIDE = 128
NBLK = 64
FD = 4
TT = 8
MAXT = 3
WMAX = 8
SPB = 64
FIRST = 4
CHUNK = 16
GROUP = 8
AHEAD = 3
HALF = SIDE // 2
FR = 72
FS = 80
BACK = 128 - TT
MESH = pl.DeviceIdType.MESH
F32 = jnp.float32
BF16 = jnp.bfloat16
FT = BF16


def tables(channels):
    i = np.arange(SIDE)
    ang = (i[:, None] * i[None, :] % SIDE) * (2.0 * math.pi / SIDE)
    c, s = np.cos(ang), np.sin(ang)
    w1 = np.concatenate([c[:HALF], s[:HALF], c[HALF:FR], s[HALF:FR]], 0)
    w2 = np.block([[c, -s], [-s, -c]])
    tw = (i[:, None] * i[None, :] % channels) * (2.0 * math.pi / channels)
    twiddle = np.stack([np.cos(tw[:FR]), np.sin(tw[:FR])]).astype(np.float32)
    return jnp.asarray(w1, BF16), jnp.asarray(w2, BF16), jnp.asarray(twiddle[:, :HALF], BF16), jnp.asarray(twiddle[:, HALF:])


def fine_rows(groups, width):
    g = np.arange(groups)[:, None]
    i = np.arange(width)[None, :]
    fine = g * FD * (width - 1 - i) // (groups * (width - 1))
    hot = np.stack([fine == step for step in range(FD)])
    hot = hot.reshape(FD, groups, width // SIDE, SIDE).transpose(2, 0, 1, 3)
    out = np.zeros((2, 2, FD, groups, FR))
    out[0, ..., : HALF + 1] = hot[..., : HALF + 1]
    out[1, ..., 1:HALF] = hot[..., : HALF : -1]
    return jnp.asarray(out.reshape(-1, FR), BF16)


def iota(shape, dim):
    return lax.broadcasted_iota(jnp.int32, shape, dim)


def search_kernel(
    sizes, raw_ref, proto_ref, w1_any, w2_any, tw_any, last_any, m_any, delays_any, widths_any, owners_any, out_ref,
    xbuf, proto, w1_ref, w2_ref, tw_ref, last_ref, m_ref, delays_ref, widths_ref, owners_ref,
    yone, ytwo, hist_raw, hist_out, history, p_ref, band_ref, band_out, bands, inv, direct, mirror, send, sendb, got, gotb,
    masks, pack_ref, kernel_ref, root_ref, open_sem, raw_sem, proto_sem, const_sem,
    hist_send, hist_recv, band_send, band_recv, own_send, own_recv, next_send, next_recv,
):
    spectra, spec, groups, slabs, owner_count, axes = sizes
    frame = SIDE * SIDE
    slots = out_ref.shape[0]
    boxes = widths_ref.shape[1]
    trials = out_ref.shape[2] // boxes
    quad = trials * groups
    rows = slots * trials
    tm, dm = lax.axis_index("tm"), lax.axis_index("dm")

    def peer(slab, owner):
        place = {name: lax.axis_index(name) for name in axes}
        place["tm"] = lax.rem(tm + slab, slabs)
        place["dm"] = lax.rem(dm + owner, owner_count)
        return tuple(place[name] for name in axes)

    def remote(src, dst, send_sem, recv_sem, target):
        return pltpu.make_async_remote_copy(
            src_ref=src, dst_ref=dst, send_sem=send_sem, recv_sem=recv_sem,
            device_id=target, device_id_type=MESH,
        )

    def raw_copy(piece):
        start = pl.multiple_of(piece * CHUNK * frame, CHUNK * frame)
        return pltpu.make_async_copy(
            raw_ref.at[:, pl.ds(start, CHUNK * frame)],
            xbuf.at[:, pl.ds(start + 3 * frame, CHUNK * frame)],
            raw_sem.at[piece],
        )

    def opening(half):
        start = half * CHUNK // 2 * frame
        return pltpu.make_async_copy(
            raw_ref.at[:, pl.ds(start, CHUNK // 2 * frame)],
            xbuf.at[:, pl.ds(start + 3 * frame, CHUNK // 2 * frame)],
            open_sem.at[half],
        )

    def history_copy():
        return remote(hist_out, history, hist_send, hist_recv, peer(1, 0))

    ending = pltpu.make_async_copy(
        raw_ref.at[:, pl.ds((spec - 3) * frame, 3 * frame)], hist_raw, open_sem.at[2]
    )
    if slabs > 1:
        ending.start()
    taps = [
        pltpu.make_async_copy(proto_ref.at[tap : tap + 1], proto.at[tap], proto_sem.at[tap])
        for tap in range(4)
    ]
    opening(0).start()
    for copy in taps:
        copy.start()
    opening(1).start()
    barrier = pltpu.get_barrier_semaphore()
    senders = [(off, 0) for off in range(1, slabs)] + [(0, off) for off in range(1, owner_count)]
    if slabs > 1:
        senders += [(slabs - 1, off) for off in range(1, owner_count)]
    for slab, owner in senders:
        pl.semaphore_signal(barrier, inc=1, device_id=peer(slab, owner), device_id_type=MESH)

    constants = [
        pltpu.make_async_copy(src, dst, const_sem.at[n])
        for n, (src, dst) in enumerate(
            [
                (w1_any, w1_ref), (tw_any, tw_ref), (last_any, last_ref), (w2_any, w2_ref), (m_any, m_ref),
                (delays_any, delays_ref), (widths_any, widths_ref), (owners_any, owners_ref),
            ]
        )
    ]
    constants[0].start()
    constants[1].start()
    constants[2].start()
    constants[3].start()
    raw_copy(1).start()
    for copy in constants[4:]:
        copy.start()
    for piece in range(2, AHEAD):
        raw_copy(piece).start()
    band_ref[...] = jnp.zeros_like(band_ref)
    xbuf[:, : 3 * frame] = jnp.zeros((1, 3 * frame), BF16)

    tile = 16 * SIDE

    def fir(ybuf, base, tiles, first=0, last=CHUNK, past=False):
        for r in tiles:
            taps = [proto[tap, :, r * tile : (r + 1) * tile].reshape(16, SIDE).astype(FT) for tap in range(4)]
            seen = []
            for k in range(first - 3, last):
                if past and k < 0:
                    row = (k + 3) * SIDE + r * 16
                    seen.append(jnp.where(tm > 0, history[row : row + 16].astype(F32), 0.0).astype(FT))
                    continue
                start = pl.multiple_of((base + k + 3) * frame + r * tile, tile)
                seen.append(xbuf[:, pl.ds(start, tile)].reshape(16, SIDE).astype(FT))
                if k >= first:
                    acc = (seen[-4] * taps[0] + seen[-3] * taps[1]) + (seen[-2] * taps[2] + seen[-1] * taps[3])
                    ybuf[k // 2, r * 16 : (r + 1) * 16, k % 2 * SIDE : (k % 2 + 1) * SIDE] = acc.astype(BF16)

    def dots(ybuf, base, s, count, keep=None):
        ts = []
        for p in range(s // 2, s // 2 + count):
            a = jnp.dot(w1_ref[...], ybuf[p], preferred_element_type=F32)
            res, ims, tails = [], [], []
            for m in range(2):
                part = a[:, m * SIDE : (m + 1) * SIDE]
                re, im = part[:HALF].astype(BF16), part[HALF : 2 * HALF].astype(BF16)
                res.append(re * tw_ref[0] - im * tw_ref[1])
                ims.append(im * tw_ref[0] + re * tw_ref[1])
                re, im = part[2 * HALF : HALF + FR], part[HALF + FR :]
                tails.append((re * last_ref[0] - im * last_ref[1], im * last_ref[0] + re * last_ref[1]))
            for n, parts in enumerate((res, ims)):
                parts.append(jnp.concatenate([tail[n] for tail in tails], 0).astype(BF16))
            ts.append(jnp.concatenate([jnp.concatenate(res, 0), jnp.concatenate(ims, 0)], 1))
        c = jnp.dot(jnp.concatenate(ts, 0), w2_ref[...], preferred_element_type=F32)
        re, im = c[:, :SIDE], c[:, SIDE:]
        power = re * re + im * im
        parts = []
        for k in range(2 * count):
            top = k // 2 * 2 * FR
            head = top + k % 2 * HALF
            tail = top + 2 * HALF + k % 2 * (FR - HALF)
            parts.append(jnp.concatenate([power[head : head + HALF], power[tail : tail + FR - HALF]], 0))
            p_ref[pl.ds(pl.multiple_of((base + s + k) * FR, FR), FR)] = parts[-1]
        if keep is not None:
            parts[:FIRST] = [jnp.where(keep, part, 0.0) for part in parts[:FIRST]]
        while len(parts) > 1:
            parts = [parts[k] + parts[k + 1] for k in range(0, len(parts), 2)]
        band_ref[...] += parts[0]

    def stage(ybuf, base, ynext, following, keep=None):
        units = CHUNK // (2 * GROUP)
        for u in range(units):
            dots(ybuf, base, 2 * GROUP * u, GROUP, keep if u == 0 else None)
            fir(ynext, following, range(8 * u // units, 8 * (u + 1) // units))

    if slabs > 1:
        ending.wait()
        hist_out[...] = hist_raw[...].reshape(3 * SIDE, SIDE)
    opening(0).wait()
    for copy in taps:
        copy.wait()
    raw_copy(AHEAD).start()
    fir(yone, 0, range(8), 0, CHUNK // 2)
    pl.semaphore_wait(barrier, len(senders))
    if slabs > 1:
        history_copy().start()
    opening(1).wait()
    fir(yone, 0, range(8), CHUNK // 2, CHUNK)
    for copy in constants[:4]:
        copy.wait()

    def chunk(step, carry):
        base = step * (2 * CHUNK)

        def arrive(piece):
            raw_copy(piece).wait()

            @pl.when(piece + AHEAD < pieces)
            def _():
                raw_copy(piece + AHEAD).start()

        arrive(2 * step + 1)
        arrive(2 * step + 2)

        stage(yone, base, ytwo, base + CHUNK, step > 0)
        stage(ytwo, base + CHUNK, yone, base + 2 * CHUNK)
        return carry

    pieces = spec // CHUNK
    steps = pieces // 2
    lax.fori_loop(0, steps - 1, chunk, 0)
    base = spec - 2 * CHUNK
    raw_copy(pieces - 1).wait()
    stage(yone, base, ytwo, base + CHUNK)
    if slabs > 1:
        history_copy().wait()
    fir(yone, 0, range(8), 0, FIRST, slabs > 1)
    for s in range(0, CHUNK, 2 * GROUP):
        dots(ytwo, base + CHUNK, s, GROUP)
    dots(yone, 0, 0, FIRST // 2)

    band_out[...] = jnp.concatenate([band_ref[...], jnp.zeros((FS - FR, SIDE), F32)], 0).astype(BF16)
    copies = []
    for off in range(1, slabs):
        copy = remote(band_out, bands.at[off - 1], band_send.at[off - 1], band_recv.at[off - 1], peer(off, 0))
        copy.start()
        copies.append(copy)

    for copy in constants[4:]:
        copy.wait()
    lanes = (MAXT + 1) * quad
    spot = iota((NBLK, SIDE), 0)
    lane = iota((NBLK, SIDE), 1) // 2
    spread = jnp.concatenate([lane == spot, lane == NBLK - 1 - spot], 1).astype(F32).astype(BF16)
    late = jnp.dot(delays_ref[...].astype(F32).astype(BF16), spread, preferred_element_type=F32)
    line = iota((quad, 2 * SIDE), 0) // trials
    for g in range(groups):
        masks[g] = jnp.concatenate(
            [
                jnp.where((late == float(v)) & (line == g), 1.0, 0.0)
                for v in range(MAXT + 1)
            ],
            0,
        ).astype(BF16)

    def column(ref):
        n = ref.shape[1]
        same = iota((n, n), 0) == iota((n, n), 1)
        return jnp.sum(jnp.where(same, jnp.broadcast_to(ref[...], (n, n)), 0), 1, keepdims=True)

    lane = iota((groups, lanes), 1) % quad
    row = iota((groups, lanes), 0)
    owner = jnp.broadcast_to(column(owners_ref), (groups, lanes))
    mine = jnp.sum(jnp.where(lane // trials == row, owner, 0), 0, keepdims=True)
    rank = jnp.sum(jnp.where((owner == mine) & (row < lane // trials), 1, 0), 0, keepdims=True)
    place = (mine * slots + rank) * trials + lane[:1] % trials
    pack = jnp.where(iota((owner_count * rows, lanes), 0) == place, 1.0, 0.0)
    pack_ref[...] = jnp.concatenate([pack, pack], 1).astype(BF16)

    reach = jnp.broadcast_to(column(widths_ref), (boxes, SIDE))
    root = 1.0 / jnp.sqrt(reach.astype(F32))
    root_ref[...] = jnp.concatenate([root] * rows, 0)
    reach = jnp.concatenate([reach] * rows, 0)
    if WMAX * rows > SIDE:
        reach = jnp.broadcast_to(reach[:, :1], (boxes * rows, WMAX * rows))
    lag = iota((boxes * rows, WMAX * rows), 1)
    series = iota((boxes * rows, WMAX * rows), 0) // boxes
    kernel = jnp.where((lag % rows == series) & (lag // rows < reach), 1.0, 0.0)
    kernel_ref[...] = kernel.astype(BF16)
    used = (spec + FD - 1) * groups
    direct[used:] = jnp.zeros((direct.shape[0] - used, SIDE), F32)
    mirror[used:] = jnp.zeros((direct.shape[0] - used, SIDE), F32)

    band = band_ref[...]
    for off in range(1, slabs):
        copies[off - 1].wait()
        band = band + bands[off - 1].astype(F32)[:FR]
    scale = 1.0 / (4 * frame)
    held = iota((FR, SIDE), 0) <= HALF
    inv[...] = jnp.where(held, scale / (band * (scale / spectra) + 1e-06), 0.0)

    even = iota((FD * groups, SIDE), 1) % 2 == 0
    size = FD * groups

    def flat(step, k):
        ratio = p_ref[pl.ds(pl.multiple_of((step * SPB + k) * FR, FR), FR)] * inv[...]
        total = 2.0 * jnp.sum(ratio, 0, keepdims=True) - ratio[:1] - ratio[HALF : HALF + 1]
        mean = jnp.sum(total, 1, keepdims=True) * (1.0 / frame)
        return (ratio - mean).astype(BF16)

    def block(step, carry):
        carry = list(carry)
        for s in range(0, SPB, 2):
            flats = jnp.concatenate([flat(step, s), flat(step, s + 1)], 1)
            r = jnp.dot(m_ref[...], flats, preferred_element_type=F32)
            for m in range(2):
                part = r[:, m * SIDE : (m + 1) * SIDE]
                one = jnp.where(even, part[:size], part[size : 2 * size])
                two = jnp.where(even, part[3 * size :], part[2 * size : 3 * size])
                for n, (ref, new) in enumerate(((direct, one), (mirror, two))):
                    new = [new[d * groups : (d + 1) * groups] for d in range(FD)]
                    held = carry[n * (FD - 1) : (n + 1) * (FD - 1)] + [0.0]
                    at = pl.multiple_of((step * SPB + s + m) * groups, groups)
                    ref[pl.ds(at, groups)] = held[0] + new[0]
                    for d in range(1, FD):
                        carry[n * (FD - 1) + d - 1] = held[d] + new[d]
        return tuple(carry)

    def sweep(first, last):
        zero = jnp.zeros((groups, SIDE), F32)
        return lax.fori_loop(first, last, block, (zero,) * (2 * (FD - 1)))

    def series(first, count):
        each = 0.0
        for g in range(groups):
            picked = pl.ds(first * groups + g, count, stride=groups)
            both = jnp.concatenate([direct[picked, :], mirror[picked, :]], 1).astype(BF16)
            each = each + lax.dot_general(
                both, masks[g], (((1,), (1,)), ((), ())), preferred_element_type=F32
            )
        return each * (1.0 / math.sqrt(SIDE * SIDE // NBLK) / math.sqrt(NBLK))

    def gather(each, skip, count):
        length = skip + count
        padded = each
        if length > each.shape[0]:
            padded = jnp.concatenate([each, jnp.zeros((length - each.shape[0], lanes), F32)], 0)
        value = iota((count, lanes), 1) // quad
        dd = 0.0
        for v in range(MAXT + 1):
            start = skip - v * TT
            if start < 0:
                moved = jnp.concatenate([jnp.zeros((-start, lanes), F32), padded[: count + start]], 0)
            else:
                moved = padded[start : start + count]
            dd = jnp.where(value == v, moved, dd)
        if count < SIDE:
            dd = jnp.concatenate([dd, jnp.zeros((SIDE - count, lanes), F32)], 0)
        high = dd.astype(BF16)
        low = (dd - high.astype(F32)).astype(BF16)
        return lax.dot_general(
            pack_ref[...], jnp.concatenate([high, low], 1), (((1,), (1,)), ((), ())), preferred_element_type=F32
        )

    blocks = spec // SPB
    middle = blocks // 2
    count = direct.shape[0] // groups
    carry = sweep(middle, blocks)
    for d in range(FD - 1):
        direct[(spec + d) * groups : (spec + d + 1) * groups] = carry[d]
        mirror[(spec + d) * groups : (spec + d + 1) * groups] = carry[FD - 1 + d]
    copies = []
    half = middle * SPB
    upper = series(half, count - half)
    if slabs > 1:
        reach = (MAXT + 1) * TT
        late = upper[spec - reach - half :]
        sendb[...] = gather(late, reach - TT, count - spec + reach).reshape(sendb.shape).astype(BF16)
        for off in range(owner_count - 1, -1, -1):
            copy = remote(
                sendb.at[lax.rem(dm + off, owner_count)], gotb.at[dm],
                next_send.at[off], next_recv.at[off], peer(1, off),
            )
            copy.start()
            copies.append(copy)
    carry = sweep(0, middle)
    for d in range(FD - 1):
        start = (middle * SPB + d) * groups
        direct[start : start + groups] += carry[d]
        mirror[start : start + groups] += carry[FD - 1 + d]
    lower = series(0, half + 16)
    each = jnp.concatenate([lower, upper[16 : spec - half]], 0)
    send[...] = gather(each, 0, spec).reshape(send.shape).astype(BF16)
    for off in range(1, owner_count):
        copy = remote(
            send.at[lax.rem(dm + off, owner_count)], got.at[dm],
            own_send.at[off - 1], own_recv.at[off - 1], peer(0, off),
        )
        copy.start()
        copies.append(copy)
    got[dm] = send[dm]
    for copy in copies:
        copy.wait()

    lane = iota((rows, SIDE), 1)
    stacks = []
    for d in range(owner_count):
        own = got[d].astype(F32)
        if slabs > 1:
            past = pltpu.roll(jnp.where(tm > 0, gotb[d].astype(F32), 0.0), SIDE - TT, 1)
            own = own + jnp.where(lane < SIDE - TT, past, 0.0)
        else:
            past = jnp.zeros((rows, SIDE), F32)
        moved = [own]
        for lag in range(1, WMAX):
            moved.append(pltpu.roll(jnp.where(lane < SIDE - lag, own, past), lag, 1))
        stacks.append(jnp.concatenate(moved, 0))
    stack = jnp.concatenate(stacks, 1).astype(BF16)
    box = jnp.dot(kernel_ref[...], stack, preferred_element_type=F32)
    for d in range(owner_count):
        done = (box[:, d * SIDE : (d + 1) * SIDE] * root_ref[...]).astype(BF16)
        for s in range(slots):
            out_ref[s, d] = done[s * trials * boxes : (s + 1) * trials * boxes]


def shards(axes, raw, proto, delays, widths, owners):
    taps, channels = proto.shape
    spec = raw.shape[1] // channels
    groups, trials, _ = delays.shape
    slabs, owner_count = lax.axis_size("tm"), lax.axis_size("dm")
    capacity = 2 * (groups // owner_count)
    w1, w2, tw, last = tables(channels)
    masks = fine_rows(groups, channels // NBLK)
    sizes = (spec * slabs, spec, groups, slabs, owner_count, axes)
    rows = -(-(spec + FD - 1) // 8) * 8
    lanes = (MAXT + 1) * groups * trials
    boxes = widths.shape[0]
    block = pltpu.VMEM((owner_count, capacity * trials, SIDE), BF16)
    sems = lambda n: pltpu.SemaphoreType.DMA((max(n, 1),))
    small = [w1, w2, tw, last, masks, delays.reshape(groups * trials, NBLK), widths[None], owners.T]
    out = (capacity, owner_count, trials * widths.shape[0], spec)
    box = pl.pallas_call(
        functools.partial(search_kernel, sizes),
        in_specs=[pl.BlockSpec(memory_space=pl.ANY)] * (2 + len(small)),
        out_specs=pl.BlockSpec(memory_space=pltpu.VMEM),
        out_shape=pltpu.VMEM(out, BF16),
        scratch_shapes=[
            pltpu.VMEM((1, (spec + 3) * channels), BF16),
            pltpu.VMEM((taps, 1, channels), F32),
            *[pltpu.VMEM(value.shape, value.dtype) for value in small],
            pltpu.VMEM((CHUNK // 2, SIDE, 2 * SIDE), BF16),
            pltpu.VMEM((CHUNK // 2, SIDE, 2 * SIDE), BF16),
            pltpu.VMEM((1, 3 * channels), BF16),
            pltpu.VMEM((3 * SIDE, SIDE), BF16),
            pltpu.VMEM((3 * SIDE, SIDE), BF16),
            pltpu.VMEM((spec * FR, SIDE), F32),
            pltpu.VMEM((FR, SIDE), F32),
            pltpu.VMEM((FS, SIDE), BF16),
            pltpu.VMEM((max(slabs - 1, 1), FS, SIDE), BF16),
            pltpu.VMEM((FR, SIDE), F32),
            pltpu.VMEM((rows * groups, SIDE), F32),
            pltpu.VMEM((rows * groups, SIDE), F32),
            block,
            block,
            block,
            block,
            pltpu.VMEM((groups, lanes, 2 * SIDE), BF16),
            pltpu.VMEM((owner_count * capacity * trials, 2 * lanes), BF16),
            pltpu.VMEM((boxes * capacity * trials, WMAX * capacity * trials), BF16),
            pltpu.VMEM((boxes * capacity * trials, SIDE), F32),
            sems(3),
            sems(spec // CHUNK),
            sems(taps),
            sems(len(small)),
            pltpu.SemaphoreType.DMA,
            pltpu.SemaphoreType.DMA,
            sems(slabs - 1),
            sems(slabs - 1),
            sems(owner_count - 1),
            sems(owner_count - 1),
            sems(owner_count),
            sems(owner_count),
        ],
        compiler_params=pltpu.CompilerParams(
            vmem_limit_bytes=56 << 20, collective_id=0, has_side_effects=True
        ),
        name="search",
    )(raw, proto, *small)
    return box.reshape(capacity, owner_count, 1, trials, widths.shape[0], spec)


def solution(mesh):
    return jax.shard_map(
        functools.partial(shards, mesh.axis_names),
        mesh=mesh,
        in_specs=(P(("group", "dm", "beam"), "tm"), P(), P(), P(), P()),
        out_specs=P("dm", "group", "beam", None, None, "tm"),
        check_vma=False,
    )
```
